128 devices in a mesh: sensor: 16 (over z, x), partner: 8 (over y, core).
Axes of the slice: x: 4, y: 4, z: 4, core: 2. Of those that a mesh axis runs over, the one named last changes fastest.
Arguments:
- spectra: bfloat16 [2048, 3, 2, 512], P(('sensor', 'partner')), may hold values from -6 to 6
- pair_slot: int32 [2048, 128], P(('sensor', 'partner')), may hold values from 0 to 255, as said below
- slot_cell: int32 [16, 256], replicated, may hold values from -1 to 4095, as said below
- cell_rank: int32 [4096], replicated, may hold values from 0 to 4095, as said below
Outputs:
- correlations: bfloat16 [4096, 9, 1024], P(('sensor', 'partner'))
The draws below stay inside these ranges and needn't reach their ends.
Inputs may be any that keep to these rules, and one draw needn't show every extreme that they name: `cell_rank`: A permutation of the cell numbers; the device of mesh index d (sensor index times 8 plus partner index) owns the cells of rank d * 32 to (d + 1) * 32 - 1. `slot_cell`: row g holds the cells of sensor group g's slots in blocks of 2 per device in mesh order; every cell in device d's block is owned by device d; -1 marks an unused slot; cells in one block are distinct and unused slots come last in it; in every draw some device's block is full in every row. `pair_slot`: entry [i, j] is the slot, in the row of sensor i's group, that takes the pair of sensor i and the j-th sensor of its group; it never names an unused slot.
All inputs are finite; a program needn't handle non-finite values.
Results may differ from the reference program's by a relative error of at most 0.011.
Values may be sent and summed in bfloat16 or wider, within the bound.
A program may use at most 128 MiB of HBM per device.

```python
import math
import jax
import jax.numpy as jnp
from jax import lax

LAGS = 1024
FREQS = 512
CELLS = 4096
SENS_DEV = 16
CAPQ = 2
BLOCKS = 8
GROUPS = 16
GROUP = 128
SENSORS = 2048
SLOTS = 256
CELLS_DEV = 32


def shared_tables(key):
    cell_rank = jax.random.permutation(jax.random.fold_in(key, 11), CELLS).astype(jnp.int32)
    inverse = jnp.argsort(cell_rank, stable=True).astype(jnp.int32)
    counts = jax.random.randint(jax.random.fold_in(key, 12), (GROUPS, SLOTS // CAPQ), 0, CAPQ + 1)
    filled = jax.random.randint(jax.random.fold_in(key, 13), (), 0, SLOTS // CAPQ)
    owners = jnp.arange(SLOTS // CAPQ, dtype=jnp.int32)
    counts = jnp.where(owners[None, :] == filled, CAPQ, counts)
    scores = jax.random.randint(jax.random.fold_in(key, 14), (GROUPS, SLOTS // CAPQ, CELLS_DEV), 0, 1 << 20)
    scores = scores * CELLS_DEV + jnp.arange(CELLS_DEV, dtype=jnp.int32)[None, None, :]
    local = jnp.argsort(scores, axis=2, stable=True)[:, :, :CAPQ].astype(jnp.int32)
    position = owners[None, :, None] * CELLS_DEV + local
    cells = jnp.take(inverse, position)
    within = jnp.arange(CAPQ, dtype=jnp.int32)[None, None, :]
    cells = jnp.where(within < counts[:, :, None], cells, -1)
    return (cell_rank, cells.reshape(GROUPS, SLOTS).astype(jnp.int32))


def draw_cell_rank(key, part):
    return shared_tables(key)[0]


def draw_slot_cell(key, part):
    return shared_tables(key)[1]


def draw_pair_slot(key, part):
    slot_cell = shared_tables(key)[1]
    unused = (slot_cell < 0).astype(jnp.int32)
    ordering = jnp.argsort(unused, axis=1, stable=True).astype(jnp.int32)
    used = jnp.sum(1 - unused, axis=1)
    picks = jax.random.randint(jax.random.fold_in(key, 41), (SENSORS, GROUP), 0, 1 << 20)
    group_of = jnp.arange(SENSORS, dtype=jnp.int32) // GROUP
    index = picks % used[group_of][:, None]
    return jnp.take_along_axis(ordering[group_of], index, axis=1).astype(jnp.int32)


def block_scale(key, dims, split, smallest, top_value):
    def one(axis_at, shards_of):
        heights = jax.random.uniform(jax.random.fold_in(jax.random.fold_in(key, 6), axis_at), (shards_of,), jnp.float32, smallest / len(split), top_value / len(split))
        return jnp.repeat(jnp.exp(heights), dims[axis_at] // shards_of).reshape((-1,) + (1,) * (len(dims) - axis_at - 1))

    loudness = one(*split[0])
    for cut in split[1:]:
        loudness = loudness * one(*cut)
    return loudness


def scatter_about(key, extent, scale, most, pieces=(), kind=jnp.bfloat16):
    values = scale * jax.random.normal(key, extent, jnp.float32)
    if pieces:
        values = values * block_scale(key, extent, pieces, -0.22, 0.18)
    return jnp.clip(values, -most, most).astype(kind)


def setup_inputs(seed: int = 0) -> dict:
    keys = jax.random.split(jax.random.key(seed), 5)
    spectra = scatter_about(keys[0], (SENSORS, 3, 2, FREQS), 1.0, 6.0, ((0, 128),))
    pair_slot = draw_pair_slot(jax.random.fold_in(keys[4], 71), 0)
    slot_cell = draw_slot_cell(jax.random.fold_in(keys[4], 71), 0)
    cell_rank = draw_cell_rank(jax.random.fold_in(keys[4], 71), 0)
    return {"spectra": spectra, "pair_slot": pair_slot, "slot_cell": slot_cell, "cell_rank": cell_rank}


def cross_spectra(resident, partners):
    res_real = resident[:, :, 0, :].astype(jnp.float32)
    res_imag = resident[:, :, 1, :].astype(jnp.float32)
    par_real = partners[:, :, 0, :].astype(jnp.float32)
    par_imag = partners[:, :, 1, :].astype(jnp.float32)
    left_real = res_real[:, None, :, None, :]
    left_imag = res_imag[:, None, :, None, :]
    right_real = par_real[None, :, None, :, :]
    right_imag = par_imag[None, :, None, :, :]
    real_part = left_real * right_real + left_imag * right_imag
    imag_part = left_imag * right_real - left_real * right_imag
    joined = jnp.stack([real_part, imag_part], axis=4)
    return joined.reshape(resident.shape[0] * partners.shape[0], -1).astype(jnp.bfloat16)


def lag_table(freqs, lags):
    bins = jnp.arange(freqs, dtype=jnp.int32)[:, None]
    shifts = jnp.arange(lags, dtype=jnp.int32)[None, :] - lags // 2
    phase = jnp.mod(bins * shifts, lags).astype(jnp.float32)
    angle = phase * (2.0 * math.pi / lags)
    return jnp.concatenate([jnp.cos(angle), -jnp.sin(angle)], axis=0) / freqs


def reference(spectra, pair_slot, slot_cell, cell_rank):
    width = 18 * FREQS

    def add_device(block, total):
        group_index = block // BLOCKS
        resident = lax.dynamic_slice_in_dim(spectra, block * SENS_DEV, SENS_DEV, 0)
        partners = lax.dynamic_slice_in_dim(spectra, group_index * GROUP, GROUP, 0)
        slots = lax.dynamic_slice_in_dim(pair_slot, block * SENS_DEV, SENS_DEV, 0).reshape(-1)
        products = lax.optimization_barrier(cross_spectra(resident, partners)).astype(jnp.float32)
        partial_value = jax.ops.segment_sum(products, slots, num_segments=SLOTS)
        partial_value = lax.optimization_barrier(partial_value.astype(jnp.bfloat16)).astype(jnp.float32)
        cells = lax.dynamic_index_in_dim(slot_cell, group_index, 0, keepdims=False)
        targets = jnp.where(cells >= 0, cells, CELLS).astype(jnp.int32)
        return total + jax.ops.segment_sum(partial_value, targets, num_segments=CELLS + 1)

    total = lax.fori_loop(0, SENSORS // SENS_DEV, add_device, jnp.zeros((CELLS + 1, width), jnp.float32))
    ordering = jnp.argsort(cell_rank, stable=True).astype(jnp.int32)
    ordered = jnp.take(total, ordering, axis=0)
    stacked = ordered.reshape(CELLS, 9, 2 * FREQS)
    table = lag_table(FREQS, LAGS)
    result = jnp.einsum("cax,xt->cat", stacked, table, precision=lax.Precision.HIGHEST)
    return result.astype(jnp.bfloat16)
```

```python
import functools
import math

import jax
import jax.numpy as jnp
import numpy as np
from jax import lax
from jax.experimental import pallas as pl
from jax.experimental.pallas import tpu as pltpu
from jax.sharding import PartitionSpec as P

MESH = pl.DeviceIdType.MESH
CHUNKS = (((0, 1, 2, 3), 32), ((4, 5, 6, 7), 32), ((8,), 64))


def lag_table(freqs, blocks):
    lags = 2 * freqs
    bins = np.arange(freqs)[:, None]
    shifts = np.arange(lags)[None, :] - lags // 2
    angle = np.mod(bins * shifts, lags) * (2.0 * math.pi / lags)
    both = np.stack([np.cos(angle), -np.sin(angle)]) / freqs
    both = both.reshape(2, blocks, freqs // blocks, lags).transpose(1, 0, 2, 3)
    return both.reshape(2 * freqs, lags).astype(jnp.bfloat16)


def kernel(sizes, mine_ref, target_ref, table_hbm, out_ref, got, left, right_r, right_i, slots,
           selector, total, table, send_a, recv_a, send_b, recv_b, table_sem,
           x_send, x_recv, a_send, a_recv, b_send, b_recv):
    groups, blocks, rows, cells = sizes
    sensors = blocks * rows
    own_g, own_b = lax.axis_index("sensor"), lax.axis_index("partner")
    half = out_ref.shape[2] // blocks // 2

    table_copy = pltpu.make_async_copy(table_hbm, table, table_sem)
    table_copy.start()

    barrier = pltpu.get_barrier_semaphore()
    for step in range(1, blocks):
        pl.semaphore_signal(barrier, inc=1, device_id=(own_g, lax.rem(own_b + step, blocks)), device_id_type=MESH)
    for step in range(1, groups):
        pl.semaphore_signal(barrier, inc=1, device_id=(lax.rem(own_g + step, groups), own_b), device_id_type=MESH)
    pl.semaphore_wait(barrier, blocks + groups - 2)

    def bins_copy(step, source):
        to = lax.rem(own_b + step, blocks)
        return pltpu.make_async_remote_copy(
            src_ref=mine_ref.at[to], dst_ref=got.at[source], send_sem=x_send.at[step], recv_sem=x_recv.at[step],
            device_id=(own_g, to), device_id_type=MESH)

    for step in range(1, blocks):
        bins_copy(step, own_b).start()
    got[own_b] = mine_ref[own_b]
    for step in range(1, blocks):
        bins_copy(step, lax.rem(own_b - step + blocks, blocks)).wait_recv()

    low = lax.broadcasted_iota(jnp.int32, (sensors, 2 * half), 1) < half
    for a in range(3):
        x = got[:, a].reshape(sensors, 2 * half).astype(jnp.float32)
        swapped = pltpu.roll(x, half, 1)
        left[a] = x
        left[3 + a] = jnp.where(low, swapped, -swapped)
        right_r[a] = jnp.where(low, x, swapped).astype(jnp.bfloat16)
        right_i[a] = jnp.where(low, swapped, x).astype(jnp.bfloat16)
    slots[...] = got[:, 3].reshape(sensors, sensors).astype(jnp.float32)

    slot_count = selector.shape[0]
    ids = lax.broadcasted_iota(jnp.int32, (slot_count, sensors), 0).astype(jnp.float32).astype(jnp.bfloat16)

    def select(i, carried):
        row = jnp.broadcast_to(slots[pl.ds(i, 1), :], (16, sensors)).astype(jnp.bfloat16)
        row = jnp.concatenate([row] * (slot_count // 16), axis=0)
        columns = pl.ds(pl.multiple_of(i * sensors, sensors), sensors)
        selector[:, columns] = jnp.where(row == ids, jnp.bfloat16(1), jnp.bfloat16(0))
        return carried

    lax.fori_loop(0, sensors, select, 0)

    def slot_sums(chunk, per_step, width):
        def add(step, carried):
            blocks_of = []
            for u in range(per_step):
                i = step * per_step + u
                row = {}
                for a in sorted({c // 3 for c in chunk}):
                    for part in (a, 3 + a):
                        wide = jnp.broadcast_to(left[part, pl.ds(i, 1), :], (16, 2 * half)).astype(jnp.bfloat16)
                        row[part] = jnp.concatenate([wide] * (sensors // 16), axis=0)
                terms = [row[c // 3] * right_r[c % 3] + row[3 + c // 3] * right_i[c % 3] for c in chunk]
                blocks_of.append(jnp.concatenate(terms, axis=1))
            products = jnp.concatenate(blocks_of, axis=0)
            columns = pl.ds(pl.multiple_of(step * per_step * sensors, per_step * sensors), per_step * sensors)
            total[:, :width] += jnp.dot(selector[:, columns], products, preferred_element_type=jnp.float32)
            return carried

        total[:, :width] = jnp.zeros((slot_count, width), jnp.float32)
        lax.fori_loop(0, sensors // per_step, add, 0)

    spans = []
    first = 0
    for chunk, _ in CHUNKS:
        spans.append((first, 2 * half * len(chunk)))
        first += 2 * half * len(chunk)
    share = slot_count // groups

    def sums_copy(k, step, source):
        start, width = spans[k]
        to = lax.rem(own_g + step, groups)
        return pltpu.make_async_remote_copy(
            src_ref=send_a.at[pl.ds(pl.multiple_of(to * share, share), share), pl.ds(start, width)],
            dst_ref=recv_a.at[pl.ds(pl.multiple_of(source * share, share), share), pl.ds(start, width)],
            send_sem=a_send.at[k, step], recv_sem=a_recv.at[k, step],
            device_id=(to, own_b), device_id_type=MESH)

    def start_sums(k):
        start, width = spans[k]
        send_a[:, start:start + width] = total[:, :width].astype(jnp.bfloat16)
        for step in range(1, groups):
            sums_copy(k, step, own_g).start()
        own = pl.ds(pl.multiple_of(own_g * share, share), share)
        recv_a[own, start:start + width] = send_a[own, start:start + width]

    def cells_copy(k, step, source):
        start, width = spans[k]
        to = lax.rem(own_b + step, blocks)
        return pltpu.make_async_remote_copy(
            src_ref=send_b.at[to, :, pl.ds(start, width)],
            dst_ref=recv_b.at[source, :, pl.ds(start, width)],
            send_sem=b_send.at[k, step], recv_sem=b_recv.at[k, step],
            device_id=(own_g, to), device_id_type=MESH)

    def start_cells(k):
        start, width = spans[k]
        for step in range(1, groups):
            sums_copy(k, step, lax.rem(own_g - step + groups, groups)).wait_recv()
        count = blocks * cells
        hit = lax.broadcasted_iota(jnp.int32, (count, groups * share), 0) == target_ref[...]
        matches = jnp.where(hit, 1.0, 0.0).astype(jnp.bfloat16)
        stacked = jnp.dot(matches, recv_a[:, start:start + width], preferred_element_type=jnp.float32)
        send_b[:, :, start:start + width] = stacked.astype(jnp.bfloat16).reshape(blocks, cells, width)
        for step in range(1, blocks):
            cells_copy(k, step, own_b).start()
        recv_b[own_b, :, start:start + width] = send_b[own_b, :, start:start + width]

    def transform(k):
        start, width = spans[k]
        for step in range(1, blocks):
            cells_copy(k, step, lax.rem(own_b - step + blocks, blocks)).wait_recv()
        lines = []
        for m in range(len(CHUNKS[k][0])):
            at = start + 2 * half * m
            lines.append(jnp.concatenate([recv_b[b, :, at:at + 2 * half] for b in range(blocks)], axis=1))
        spectrum = jnp.concatenate(lines, axis=0) if len(lines) > 1 else lines[0]
        lag = jnp.dot(spectrum, table[...], preferred_element_type=jnp.float32).astype(jnp.bfloat16)
        for m, c in enumerate(CHUNKS[k][0]):
            out_ref[c] = lag[m * cells:(m + 1) * cells]

    slot_sums(CHUNKS[0][0], CHUNKS[0][1], spans[0][1])
    start_sums(0)
    slot_sums(CHUNKS[1][0], CHUNKS[1][1], spans[1][1])
    start_sums(1)
    start_cells(0)
    slot_sums(CHUNKS[2][0], CHUNKS[2][1], spans[2][1])
    start_sums(2)
    start_cells(1)
    table_copy.wait()
    transform(0)
    start_cells(2)
    transform(1)
    transform(2)

    for step in range(1, blocks):
        bins_copy(step, own_b).wait_send()
    for k in range(len(CHUNKS)):
        for step in range(1, groups):
            sums_copy(k, step, own_g).wait_send()
        for step in range(1, blocks):
            cells_copy(k, step, own_b).wait_send()


def on_device(spectra, pair_slot, slot_cell, cell_rank):
    rows, _, _, freqs = spectra.shape
    groups, slot_count = slot_cell.shape
    blocks = lax.axis_size("partner")
    sensors = rows * blocks
    cells = cell_rank.shape[0] // (groups * blocks)
    own_bins = 2 * freqs // blocks
    width = 9 * own_bins
    share = slot_count // groups

    mine = spectra.reshape(rows, 3, 2, blocks, freqs // blocks).transpose(3, 1, 0, 2, 4)
    mine = mine.reshape(blocks, 3, rows, own_bins)
    ids = jnp.broadcast_to(pair_slot.astype(jnp.bfloat16)[None, None], (blocks, 1, rows, sensors))
    mine = jnp.concatenate([mine, ids], axis=1)

    own_g = lax.axis_index("sensor")
    my_cells = lax.dynamic_slice_in_dim(slot_cell, own_g * share, share, 1)
    ranks = jnp.take(cell_rank, jnp.maximum(my_cells, 0))
    target = jnp.where(my_cells >= 0, ranks - own_g * (blocks * cells), -1).reshape(1, groups * share)

    table = jnp.asarray(lag_table(freqs, blocks))
    count = len(CHUNKS)
    widest = max(len(chunk) for chunk, _ in CHUNKS) * own_bins
    vmem = pl.BlockSpec(memory_space=pltpu.VMEM)
    out = pl.pallas_call(
        functools.partial(kernel, (groups, blocks, rows, cells)),
        out_shape=jax.ShapeDtypeStruct((9, cells, 2 * freqs), jnp.bfloat16),
        in_specs=[vmem, vmem, pl.BlockSpec(memory_space=pl.ANY)],
        out_specs=vmem,
        scratch_shapes=[
            pltpu.VMEM((blocks, 4, rows, own_bins), jnp.bfloat16),
            pltpu.VMEM((6, sensors, own_bins), jnp.float32),
            pltpu.VMEM((3, sensors, own_bins), jnp.bfloat16),
            pltpu.VMEM((3, sensors, own_bins), jnp.bfloat16),
            pltpu.VMEM((sensors, sensors), jnp.float32),
            pltpu.VMEM((slot_count, sensors * sensors), jnp.bfloat16),
            pltpu.VMEM((slot_count, widest), jnp.float32),
            pltpu.VMEM((2 * freqs, 2 * freqs), jnp.bfloat16),
            pltpu.VMEM((slot_count, width), jnp.bfloat16),
            pltpu.VMEM((groups * share, width), jnp.bfloat16),
            pltpu.VMEM((blocks, cells, width), jnp.bfloat16),
            pltpu.VMEM((blocks, cells, width), jnp.bfloat16),
            pltpu.SemaphoreType.DMA,
            pltpu.SemaphoreType.DMA((blocks,)),
            pltpu.SemaphoreType.DMA((blocks,)),
            pltpu.SemaphoreType.DMA((count, groups)),
            pltpu.SemaphoreType.DMA((count, groups)),
            pltpu.SemaphoreType.DMA((count, blocks)),
            pltpu.SemaphoreType.DMA((count, blocks)),
        ],
        compiler_params=pltpu.CompilerParams(
            collective_id=0, has_side_effects=True, vmem_limit_bytes=56 * 2**20),
        name="stack_pairs",
    )(mine, target, table)
    return out.transpose(1, 0, 2)


def solution(mesh):
    in_specs = (
        P(("sensor", "partner"), None, None, None),
        P(("sensor", "partner"), None),
        P(),
        P(),
    )
    out_specs = P(("sensor", "partner"), None, None)
    return jax.shard_map(
        on_device, mesh=mesh, in_specs=in_specs, out_specs=out_specs, check_vma=False
    )
```

```python
import functools
import math

import jax
import jax.numpy as jnp
import numpy as np
from jax import lax
from jax.experimental import pallas as pl
from jax.experimental.pallas import tpu as pltpu
from jax.sharding import PartitionSpec as P

MESH = pl.DeviceIdType.MESH
CHUNKS = (((8,), 64), ((0, 1), 64), ((2, 3), 64), ((4, 5), 64), ((6, 7), 64))


def lag_table(freqs, blocks):
    lags = 2 * freqs
    bins = np.arange(freqs)[:, None]
    shifts = np.arange(lags)[None, :] - lags // 2
    angle = np.mod(bins * shifts, lags) * (2.0 * math.pi / lags)
    both = np.stack([np.cos(angle), -np.sin(angle)]) / freqs
    both = both.reshape(2, blocks, freqs // blocks, lags).transpose(1, 0, 2, 3)
    return both.reshape(2 * freqs, lags).astype(jnp.bfloat16)


def one_hot(condition):
    return jnp.where(condition, 1.0, 0.0).astype(jnp.bfloat16)


def cell_rows(slot_cell, rank_table, own_g, share, blocks, cells):
    groups, slot_count = slot_cell.shape
    span = rank_table.shape[1]
    count = groups * share
    of_slot = lax.broadcasted_iota(jnp.int32, (slot_count, count), 0)
    incoming = lax.broadcasted_iota(jnp.int32, (slot_count, count), 1)
    pick = one_hot(of_slot == own_g * share + incoming % share)
    used = slot_cell >= 0
    high = jnp.where(used, slot_cell // span, -1).astype(jnp.float32).astype(jnp.bfloat16)
    low = jnp.where(used, slot_cell % span, 0).astype(jnp.float32).astype(jnp.bfloat16)
    group = lax.broadcasted_iota(jnp.int32, (groups, count), 0)
    mine = group == lax.broadcasted_iota(jnp.int32, (groups, count), 1) // share

    def own(values):
        spread = jnp.dot(values, pick, preferred_element_type=jnp.float32)
        return jnp.sum(jnp.where(mine, spread, 0.0), axis=0, keepdims=True)

    high, low = own(high), own(low)
    place = (rank_table % cells).astype(jnp.float32).astype(jnp.bfloat16)
    low_ids = lax.broadcasted_iota(jnp.int32, (span, count), 0).astype(jnp.float32)
    spread = jnp.dot(place, one_hot(low_ids == low), preferred_element_type=jnp.float32)
    high_ids = lax.broadcasted_iota(jnp.int32, (rank_table.shape[0], count), 0).astype(jnp.float32)
    place = jnp.sum(jnp.where(high_ids == high, spread, 0.0), axis=0, keepdims=True)
    owner = lax.broadcasted_iota(jnp.int32, (1, count), 1) % share // (share // blocks)
    return jnp.where(high >= 0, place + (owner * cells).astype(jnp.float32), -1.0)


def kernel(sizes, spectra_ref, pair_slot_ref, slot_cell_ref, rank_ref, table_hbm, out_ref, mine, got, left, right_r,
           right_i, slots, selector, total, matches, table, send_a, recv_a, send_b, recv_b, table_sem,
           x_send, x_recv, a_send, a_recv, b_send, b_recv):
    groups, blocks, rows, cells = sizes
    sensors = blocks * rows
    own_g, own_b = lax.axis_index("sensor"), lax.axis_index("partner")
    half = out_ref.shape[2] // blocks // 2

    barrier = pltpu.get_barrier_semaphore()
    for step in range(1, groups):
        pl.semaphore_signal(barrier, inc=1, device_id=(lax.rem(own_g + step, groups), own_b), device_id_type=MESH)
    for step in range(1, blocks):
        pl.semaphore_signal(barrier, inc=1, device_id=(own_g, lax.rem(own_b + step, blocks)), device_id_type=MESH)
    table_copy = pltpu.make_async_copy(table_hbm, table, table_sem)
    table_copy.start()

    ids = pair_slot_ref[...].astype(jnp.float32).astype(jnp.bfloat16)
    first = lax.broadcasted_iota(jnp.int32, (rows, 2 * half), 1) < half
    for a in range(3):
        for pair in range(blocks // 2):
            lanes = slice(pair * 2 * half, (pair + 1) * 2 * half)
            real = spectra_ref[:, a, 0, lanes].astype(jnp.float32)
            imag = spectra_ref[:, a, 1, lanes].astype(jnp.float32)
            mine[2 * pair, a] = jnp.where(first, real, pltpu.roll(imag, half, 1)).astype(jnp.bfloat16)
            mine[2 * pair + 1, a] = jnp.where(first, pltpu.roll(real, half, 1), imag).astype(jnp.bfloat16)
    for b in range(blocks):
        mine[b, 3] = ids
    share = slot_cell_ref.shape[1] // groups
    at = cell_rows(slot_cell_ref[...], rank_ref[...], own_g, share, blocks, cells)
    row_ids = lax.broadcasted_iota(jnp.int32, (blocks * cells, groups * share), 0).astype(jnp.float32)
    matches[...] = one_hot(row_ids == at)
    pl.semaphore_wait(barrier, blocks + groups - 2)

    def bins_copy(step, source):
        to = lax.rem(own_b + step, blocks)
        return pltpu.make_async_remote_copy(
            src_ref=mine.at[to], dst_ref=got.at[source], send_sem=x_send.at[step], recv_sem=x_recv.at[step],
            device_id=(own_g, to), device_id_type=MESH)

    for step in range(1, blocks):
        bins_copy(step, own_b).start()
    got[own_b] = mine[own_b]
    for step in range(1, blocks):
        bins_copy(step, lax.rem(own_b - step + blocks, blocks)).wait_recv()

    low = lax.broadcasted_iota(jnp.int32, (sensors, 2 * half), 1) < half
    for a in range(3):
        x = got[:, a].reshape(sensors, 2 * half).astype(jnp.float32)
        swapped = pltpu.roll(x, half, 1)
        left[a] = x
        left[3 + a] = jnp.where(low, swapped, -swapped)
        right_r[a] = jnp.where(low, x, swapped).astype(jnp.bfloat16)
        right_i[a] = jnp.where(low, swapped, x).astype(jnp.bfloat16)
    slots[...] = got[:, 3].reshape(sensors, sensors).astype(jnp.float32)

    slot_count = selector.shape[0]
    slot_ids = lax.broadcasted_iota(jnp.int32, (slot_count, sensors), 0).astype(jnp.float32).astype(jnp.bfloat16)

    def select(i):
        row = jnp.broadcast_to(slots[pl.ds(i, 1), :], (16, sensors)).astype(jnp.bfloat16)
        row = jnp.concatenate([row] * (slot_count // 16), axis=0)
        return jnp.where(row == slot_ids, jnp.bfloat16(1), jnp.bfloat16(0))

    def slot_sums(k):
        chunk, per_step = CHUNKS[k]
        width = spans[k][1]

        def add(step, carried):
            blocks_of = []
            for u in range(per_step):
                i = step * per_step + u
                row = {}
                for a in sorted({c // 3 for c in chunk}):
                    for part in (a, 3 + a):
                        wide = jnp.broadcast_to(left[part, pl.ds(i, 1), :], (16, 2 * half)).astype(jnp.bfloat16)
                        row[part] = jnp.concatenate([wide] * (sensors // 16), axis=0)
                terms = [row[c // 3] * right_r[c % 3] + row[3 + c // 3] * right_i[c % 3] for c in chunk]
                blocks_of.append(jnp.concatenate(terms, axis=1))
            products = jnp.concatenate(blocks_of, axis=0)
            columns = pl.ds(pl.multiple_of(step * per_step * sensors, per_step * sensors), per_step * sensors)
            if k == 0:
                chosen = jnp.concatenate([select(step * per_step + u) for u in range(per_step)], axis=1)
                selector[:, columns] = chosen
            else:
                chosen = selector[:, columns]
            total[:, :width] += jnp.dot(chosen, products, preferred_element_type=jnp.float32)
            return carried

        total[:, :width] = jnp.zeros((slot_count, width), jnp.float32)
        lax.fori_loop(0, sensors // per_step, add, 0)

    spans = []
    first = 0
    for chunk, _ in CHUNKS:
        spans.append((first, 2 * half * len(chunk)))
        first += 2 * half * len(chunk)

    def sums_copy(k, step, source):
        start, width = spans[k]
        to = lax.rem(own_g + step, groups)
        return pltpu.make_async_remote_copy(
            src_ref=send_a.at[pl.ds(pl.multiple_of(to * share, share), share), pl.ds(start, width)],
            dst_ref=recv_a.at[pl.ds(pl.multiple_of(source * share, share), share), pl.ds(start, width)],
            send_sem=a_send.at[k, step], recv_sem=a_recv.at[k, step],
            device_id=(to, own_b), device_id_type=MESH)

    def start_sums(k):
        start, width = spans[k]
        send_a[:, start:start + width] = total[:, :width].astype(jnp.bfloat16)
        for step in range(1, groups):
            sums_copy(k, step, own_g).start()
        own = pl.ds(pl.multiple_of(own_g * share, share), share)
        recv_a[own, start:start + width] = send_a[own, start:start + width]

    def cells_copy(k, step, source):
        start, width = spans[k]
        to = lax.rem(own_b + step, blocks)
        return pltpu.make_async_remote_copy(
            src_ref=send_b.at[to, :, pl.ds(start, width)],
            dst_ref=recv_b.at[source, :, pl.ds(start, width)],
            send_sem=b_send.at[k, step], recv_sem=b_recv.at[k, step],
            device_id=(own_g, to), device_id_type=MESH)

    def start_cells(k):
        start, width = spans[k]
        for step in range(1, groups):
            sums_copy(k, step, lax.rem(own_g - step + groups, groups)).wait_recv()
        stacked = jnp.dot(matches[...], recv_a[:, start:start + width], preferred_element_type=jnp.float32)
        send_b[:, :, start:start + width] = stacked.astype(jnp.bfloat16).reshape(blocks, cells, width)
        for step in range(1, blocks):
            cells_copy(k, step, own_b).start()
        recv_b[own_b, :, start:start + width] = send_b[own_b, :, start:start + width]

    def transform(k):
        start, width = spans[k]
        for step in range(1, blocks):
            cells_copy(k, step, lax.rem(own_b - step + blocks, blocks)).wait_recv()
        lines = []
        for m in range(len(CHUNKS[k][0])):
            at = start + 2 * half * m
            lines.append(jnp.concatenate([recv_b[b, :, at:at + 2 * half] for b in range(blocks)], axis=1))
        spectrum = jnp.concatenate(lines, axis=0) if len(lines) > 1 else lines[0]
        lag = jnp.dot(spectrum, table[...], preferred_element_type=jnp.float32).astype(jnp.bfloat16)
        for m, c in enumerate(CHUNKS[k][0]):
            out_ref[c] = lag[m * cells:(m + 1) * cells]

    count = len(CHUNKS)
    for k in range(count):
        slot_sums(k)
        start_sums(k)
        if k >= 1:
            start_cells(k - 1)
    table_copy.wait()
    for k in range(count - 1):
        transform(k)
    start_cells(count - 1)
    transform(count - 1)

    for step in range(1, blocks):
        bins_copy(step, own_b).wait_send()
    for k in range(count):
        for step in range(1, groups):
            sums_copy(k, step, own_g).wait_send()
        for step in range(1, blocks):
            cells_copy(k, step, own_b).wait_send()


def on_device(spectra, pair_slot, slot_cell, cell_rank):
    rows, _, _, freqs = spectra.shape
    groups, slot_count = slot_cell.shape
    blocks = lax.axis_size("partner")
    sensors = rows * blocks
    cells = cell_rank.shape[0] // (groups * blocks)
    own_bins = 2 * freqs // blocks
    width = 9 * own_bins
    share = slot_count // groups

    table = jnp.asarray(lag_table(freqs, blocks))
    count = len(CHUNKS)
    widest = max(len(chunk) for chunk, _ in CHUNKS) * own_bins
    vmem = pl.BlockSpec(memory_space=pltpu.VMEM)
    out = pl.pallas_call(
        functools.partial(kernel, (groups, blocks, rows, cells)),
        out_shape=jax.ShapeDtypeStruct((9, cells, 2 * freqs), jnp.bfloat16),
        in_specs=[vmem, vmem, vmem, vmem, pl.BlockSpec(memory_space=pl.ANY)],
        out_specs=vmem,
        scratch_shapes=[
            pltpu.VMEM((blocks, 4, rows, own_bins), jnp.bfloat16),
            pltpu.VMEM((blocks, 4, rows, own_bins), jnp.bfloat16),
            pltpu.VMEM((6, sensors, own_bins), jnp.float32),
            pltpu.VMEM((3, sensors, own_bins), jnp.bfloat16),
            pltpu.VMEM((3, sensors, own_bins), jnp.bfloat16),
            pltpu.VMEM((sensors, sensors), jnp.float32),
            pltpu.VMEM((slot_count, sensors * sensors), jnp.bfloat16),
            pltpu.VMEM((slot_count, widest), jnp.float32),
            pltpu.VMEM((blocks * cells, groups * share), jnp.bfloat16),
            pltpu.VMEM((2 * freqs, 2 * freqs), jnp.bfloat16),
            pltpu.VMEM((slot_count, width), jnp.bfloat16),
            pltpu.VMEM((groups * share, width), jnp.bfloat16),
            pltpu.VMEM((blocks, cells, width), jnp.bfloat16),
            pltpu.VMEM((blocks, cells, width), jnp.bfloat16),
            pltpu.SemaphoreType.DMA,
            pltpu.SemaphoreType.DMA((blocks,)),
            pltpu.SemaphoreType.DMA((blocks,)),
            pltpu.SemaphoreType.DMA((count, groups)),
            pltpu.SemaphoreType.DMA((count, groups)),
            pltpu.SemaphoreType.DMA((count, blocks)),
            pltpu.SemaphoreType.DMA((count, blocks)),
        ],
        compiler_params=pltpu.CompilerParams(
            collective_id=0, has_side_effects=True, vmem_limit_bytes=56 * 2**20),
        name="stack_pairs",
    )(spectra, pair_slot, slot_cell, cell_rank.reshape(-1, 128), table)
    return out.transpose(1, 0, 2)


def solution(mesh):
    in_specs = (
        P(("sensor", "partner"), None, None, None),
        P(("sensor", "partner"), None),
        P(),
        P(),
    )
    out_specs = P(("sensor", "partner"), None, None)
    return jax.shard_map(
        on_device, mesh=mesh, in_specs=in_specs, out_specs=out_specs, check_vma=False
    )
```

```python
import functools
import math

import jax
import jax.numpy as jnp
import numpy as np
from jax import lax
from jax.experimental import pallas as pl
from jax.experimental.pallas import tpu as pltpu
from jax.sharding import PartitionSpec as P

MESH = pl.DeviceIdType.MESH
CHUNKS = (((0, 1, 2, 3,4,5), 32), ((6, 7,8), 32))


def lag_table(freqs, blocks):
    lags = 2 * freqs
    bins = np.arange(freqs)[:, None]
    shifts = np.arange(lags)[None, :] - lags // 2
    angle = np.mod(bins * shifts, lags) * (2.0 * math.pi / lags)
    both = np.stack([np.cos(angle), -np.sin(angle)]) / freqs
    both = both.reshape(2, blocks, freqs // blocks, lags).transpose(1, 0, 2, 3)
    return both.reshape(2 * freqs, lags).astype(jnp.bfloat16)


def one_hot(condition):
    return jnp.where(condition, 1.0, 0.0).astype(jnp.bfloat16)


def cell_rows(slot_cell, rank_table, own_g, share, blocks, cells):
    groups, slot_count = slot_cell.shape
    span = rank_table.shape[1]
    count = groups * share
    of_slot = lax.broadcasted_iota(jnp.int32, (slot_count, count), 0)
    incoming = lax.broadcasted_iota(jnp.int32, (slot_count, count), 1)
    pick = one_hot(of_slot == own_g * share + incoming % share)
    used = slot_cell >= 0
    high = jnp.where(used, slot_cell // span, -1).astype(jnp.float32).astype(jnp.bfloat16)
    low = jnp.where(used, slot_cell % span, 0).astype(jnp.float32).astype(jnp.bfloat16)
    group = lax.broadcasted_iota(jnp.int32, (groups, count), 0)
    mine = group == lax.broadcasted_iota(jnp.int32, (groups, count), 1) // share

    def own(values):
        spread = jnp.dot(values, pick, preferred_element_type=jnp.float32)
        return jnp.sum(jnp.where(mine, spread, 0.0), axis=0, keepdims=True)

    high, low = own(high), own(low)
    place = (rank_table % cells).astype(jnp.float32).astype(jnp.bfloat16)
    low_ids = lax.broadcasted_iota(jnp.int32, (span, count), 0).astype(jnp.float32)
    spread = jnp.dot(place, one_hot(low_ids == low), preferred_element_type=jnp.float32)
    high_ids = lax.broadcasted_iota(jnp.int32, (rank_table.shape[0], count), 0).astype(jnp.float32)
    place = jnp.sum(jnp.where(high_ids == high, spread, 0.0), axis=0, keepdims=True)
    owner = lax.broadcasted_iota(jnp.int32, (1, count), 1) % share // (share // blocks)
    return jnp.where(high >= 0, place + (owner * cells).astype(jnp.float32), -1.0)


def wait_for(ref, semaphore):
    pltpu.make_async_copy(ref, ref, semaphore).wait()


def kernel(sizes, spectra_hbm, pair_slot_hbm, slot_cell_hbm, rank_hbm, table_hbm, out_ref, spectra_ref, pair_slot_ref,
           slot_cell_ref, rank_ref, in_sems, mine, got, left, right_r,
           right_i, slots, total, matches, table, send_a, recv_a, send_b, recv_b, table_sem,
           x_send, x_recv, a_send, a_recv, b_send, b_recv):
    groups, blocks, rows, cells = sizes
    sensors = blocks * rows
    own_g, own_b = lax.axis_index("sensor"), lax.axis_index("partner")
    inputs = [
        pltpu.make_async_copy(source, to, in_sems.at[n])
        for n, (source, to) in enumerate((
            (spectra_hbm, spectra_ref), (pair_slot_hbm, pair_slot_ref), (slot_cell_hbm, slot_cell_ref), (rank_hbm, rank_ref)))
    ]
    for copy in inputs:
        copy.start()
    half = out_ref.shape[2] // blocks // 2

    barrier = pltpu.get_barrier_semaphore()
    for step in range(1, groups):
        pl.semaphore_signal(barrier, inc=1, device_id=(lax.rem(own_g + step, groups), own_b), device_id_type=MESH)
    for step in range(1, blocks):
        pl.semaphore_signal(barrier, inc=1, device_id=(own_g, lax.rem(own_b + step, blocks)), device_id_type=MESH)
    table_copy = pltpu.make_async_copy(table_hbm, table, table_sem)
    table_copy.start()

    for copy in inputs:
        copy.wait()
    ids = pair_slot_ref[...].astype(jnp.float32).astype(jnp.bfloat16)
    first = lax.broadcasted_iota(jnp.int32, (rows, 2 * half), 1) < half
    for a in range(3):
        for pair in range(blocks // 2):
            lanes = slice(pair * 2 * half, (pair + 1) * 2 * half)
            real = spectra_ref[:, a, 0, lanes].astype(jnp.float32)
            imag = spectra_ref[:, a, 1, lanes].astype(jnp.float32)
            mine[2 * pair, a] = jnp.where(first, real, pltpu.roll(imag, half, 1)).astype(jnp.bfloat16)
            mine[2 * pair + 1, a] = jnp.where(first, pltpu.roll(real, half, 1), imag).astype(jnp.bfloat16)
    for b in range(blocks):
        mine[b, 3] = ids
    share = slot_cell_ref.shape[1] // groups
    at = cell_rows(slot_cell_ref[...], rank_ref[...], own_g, share, blocks, cells)
    row_ids = lax.broadcasted_iota(jnp.int32, (blocks * cells, groups * share), 0).astype(jnp.float32)
    matches[...] = one_hot(row_ids == at)
    pl.semaphore_wait(barrier, blocks + groups - 2)

    def bins_copy(step):
        to = lax.rem(own_b + step, blocks)
        return pltpu.make_async_remote_copy(
            src_ref=mine.at[to], dst_ref=got.at[own_b], send_sem=x_send, recv_sem=x_recv,
            device_id=(own_g, to), device_id_type=MESH)

    for step in range(1, blocks):
        bins_copy(step).start()
    got[own_b] = mine[own_b]
    others = got.at[pl.ds(0, blocks - 1)]
    wait_for(others, x_recv)

    low = lax.broadcasted_iota(jnp.int32, (sensors, 2 * half), 1) < half
    for a in range(3):
        x = got[:, a].reshape(sensors, 2 * half).astype(jnp.float32)
        swapped = pltpu.roll(x, half, 1)
        left[a] = x
        left[3 + a] = jnp.where(low, swapped, -swapped)
        right_r[a] = jnp.where(low, x, swapped).astype(jnp.bfloat16)
        right_i[a] = jnp.where(low, swapped, x).astype(jnp.bfloat16)
    slots[...] = got[:, 3].reshape(sensors, sensors).astype(jnp.float32)

    slot_count = total.shape[0]
    slot_ids = lax.broadcasted_iota(jnp.int32, (slot_count, sensors), 0).astype(jnp.float32).astype(jnp.bfloat16)

    def select(i):
        row = jnp.broadcast_to(slots[pl.ds(i, 1), :], (16, sensors)).astype(jnp.bfloat16)
        row = jnp.concatenate([row] * (slot_count // 16), axis=0)
        return jnp.where(row == slot_ids, jnp.bfloat16(1), jnp.bfloat16(0))

    def slot_sums(k):
        chunk, per_step = CHUNKS[k]
        width = spans[k][1]

        def add(step, carried):
            blocks_of = []
            for u in range(per_step):
                i = step * per_step + u
                row = {}
                for a in sorted({c // 3 for c in chunk}):
                    for part in (a, 3 + a):
                        wide = jnp.broadcast_to(left[part, pl.ds(i, 1), :], (16, 2 * half)).astype(jnp.bfloat16)
                        row[part] = jnp.concatenate([wide] * (sensors // 16), axis=0)
                terms = [row[c // 3] * right_r[c % 3] + row[3 + c // 3] * right_i[c % 3] for c in chunk]
                blocks_of.append(jnp.concatenate(terms, axis=1))
            products = jnp.concatenate(blocks_of, axis=0)
            chosen = jnp.concatenate([select(step * per_step + u) for u in range(per_step)], axis=1)
            total[:, :width] += jnp.dot(chosen, products, preferred_element_type=jnp.float32)
            return carried

        total[:, :width] = jnp.zeros((slot_count, width), jnp.float32)
        lax.fori_loop(0, sensors // per_step, add, 0)

    spans = []
    first = 0
    for chunk, _ in CHUNKS:
        spans.append((first, 2 * half * len(chunk)))
        first += 2 * half * len(chunk)

    def sums_copy(k, step):
        start, width = spans[k]
        to = lax.rem(own_g + step, groups)
        return pltpu.make_async_remote_copy(
            src_ref=send_a.at[pl.ds(pl.multiple_of(to * share, share), share), pl.ds(start, width)],
            dst_ref=recv_a.at[pl.ds(pl.multiple_of(own_g * share, share), share), pl.ds(start, width)],
            send_sem=a_send.at[k], recv_sem=a_recv.at[k],
            device_id=(to, own_b), device_id_type=MESH)

    def start_sums(k):
        start, width = spans[k]
        send_a[:, start:start + width] = total[:, :width].astype(jnp.bfloat16)
        for step in range(1, groups):
            sums_copy(k, step).start()
        own = pl.ds(pl.multiple_of(own_g * share, share), share)
        recv_a[own, start:start + width] = send_a[own, start:start + width]

    def cells_copy(k, step):
        start, width = spans[k]
        to = lax.rem(own_b + step, blocks)
        return pltpu.make_async_remote_copy(
            src_ref=send_b.at[to, :, pl.ds(start, width)],
            dst_ref=recv_b.at[own_b, :, pl.ds(start, width)],
            send_sem=b_send.at[k], recv_sem=b_recv.at[k],
            device_id=(own_g, to), device_id_type=MESH)

    def start_cells(k):
        start, width = spans[k]
        wait_for(recv_a.at[pl.ds(0, (groups - 1) * share), pl.ds(start, width)], a_recv.at[k])
        stacked = jnp.dot(matches[...], recv_a[:, start:start + width], preferred_element_type=jnp.float32)
        send_b[:, :, start:start + width] = stacked.astype(jnp.bfloat16).reshape(blocks, cells, width)
        for step in range(1, blocks):
            cells_copy(k, step).start()
        recv_b[own_b, :, start:start + width] = send_b[own_b, :, start:start + width]

    def transform(k):
        start, width = spans[k]
        wait_for(recv_b.at[pl.ds(0, blocks - 1), :, pl.ds(start, width)], b_recv.at[k])
        lines = []
        for m in range(len(CHUNKS[k][0])):
            at = start + 2 * half * m
            lines.append(jnp.concatenate([recv_b[b, :, at:at + 2 * half] for b in range(blocks)], axis=1))
        spectrum = jnp.concatenate(lines, axis=0) if len(lines) > 1 else lines[0]
        lag = jnp.dot(spectrum, table[...], preferred_element_type=jnp.float32).astype(jnp.bfloat16)
        for m, c in enumerate(CHUNKS[k][0]):
            out_ref[c] = lag[m * cells:(m + 1) * cells]

    count = len(CHUNKS)
    for k in range(count):
        slot_sums(k)
        start_sums(k)
        if k >= 1:
            start_cells(k - 1)
    table_copy.wait()
    for k in range(count - 2):
        transform(k)
    wait_for(others, x_send)
    start_cells(count - 1)
    transform(count - 2)
    for k in range(count):
        start, width = spans[k]
        wait_for(send_a.at[pl.ds(0, (groups - 1) * share), pl.ds(start, width)], a_send.at[k])
        if k < count - 1:
            wait_for(send_b.at[pl.ds(0, blocks - 1), :, pl.ds(start, width)], b_send.at[k])
    transform(count - 1)
    start, width = spans[count - 1]
    wait_for(send_b.at[pl.ds(0, blocks - 1), :, pl.ds(start, width)], b_send.at[count - 1])


def on_device(spectra, pair_slot, slot_cell, cell_rank):
    rows, _, _, freqs = spectra.shape
    groups, slot_count = slot_cell.shape
    blocks = lax.axis_size("partner")
    sensors = rows * blocks
    cells = cell_rank.shape[0] // (groups * blocks)
    own_bins = 2 * freqs // blocks
    width = 9 * own_bins
    share = slot_count // groups

    table = jnp.asarray(lag_table(freqs, blocks))
    count = len(CHUNKS)
    widest = max(len(chunk) for chunk, _ in CHUNKS) * own_bins
    vmem = pl.BlockSpec(memory_space=pltpu.VMEM)
    out = pl.pallas_call(
        functools.partial(kernel, (groups, blocks, rows, cells)),
        out_shape=pltpu.VMEM((9, cells, 2 * freqs), jnp.bfloat16),
        in_specs=[pl.BlockSpec(memory_space=pl.ANY)] * 5,
        out_specs=vmem,
        scratch_shapes=[
            pltpu.VMEM(spectra.shape, spectra.dtype),
            pltpu.VMEM(pair_slot.shape, pair_slot.dtype),
            pltpu.VMEM(slot_cell.shape, slot_cell.dtype),
            pltpu.VMEM((cell_rank.shape[0] // 128, 128), cell_rank.dtype),
            pltpu.SemaphoreType.DMA((4,)),
            pltpu.VMEM((blocks, 4, rows, own_bins), jnp.bfloat16),
            pltpu.VMEM((blocks, 4, rows, own_bins), jnp.bfloat16),
            pltpu.VMEM((6, sensors, own_bins), jnp.float32),
            pltpu.VMEM((3, sensors, own_bins), jnp.bfloat16),
            pltpu.VMEM((3, sensors, own_bins), jnp.bfloat16),
            pltpu.VMEM((sensors, sensors), jnp.float32),
            pltpu.VMEM((slot_count, widest), jnp.float32),
            pltpu.VMEM((blocks * cells, groups * share), jnp.bfloat16),
            pltpu.VMEM((2 * freqs, 2 * freqs), jnp.bfloat16),
            pltpu.VMEM((slot_count, width), jnp.bfloat16),
            pltpu.VMEM((groups * share, width), jnp.bfloat16),
            pltpu.VMEM((blocks, cells, width), jnp.bfloat16),
            pltpu.VMEM((blocks, cells, width), jnp.bfloat16),
            pltpu.SemaphoreType.DMA,
            pltpu.SemaphoreType.DMA,
            pltpu.SemaphoreType.DMA,
            pltpu.SemaphoreType.DMA((count,)),
            pltpu.SemaphoreType.DMA((count,)),
            pltpu.SemaphoreType.DMA((count,)),
            pltpu.SemaphoreType.DMA((count,)),
        ],
        compiler_params=pltpu.CompilerParams(
            collective_id=0, has_side_effects=True, vmem_limit_bytes=56 * 2**20),
        name="stack_pairs",
    )(spectra, pair_slot, slot_cell, cell_rank.reshape(-1, 128), table)
    return out.transpose(1, 0, 2)


def solution(mesh):
    in_specs = (
        P(("sensor", "partner"), None, None, None),
        P(("sensor", "partner"), None),
        P(),
        P(),
    )
    out_specs = P(("sensor", "partner"), None, None)
    return jax.shard_map(
        on_device, mesh=mesh, in_specs=in_specs, out_specs=out_specs, check_vma=False
    )
```

```python
import functools
import math

import jax
import jax.numpy as jnp
import numpy as np
from jax import lax
from jax.experimental import pallas as pl
from jax.experimental.pallas import tpu as pltpu
from jax.sharding import PartitionSpec as P

MESH = pl.DeviceIdType.MESH
CHUNKS = (((0, 1), (0, 2)), ((1, 2), "01", "2"))
MADE = {(0, 1): (1, 3), (0, 2): (2, 6), (1, 2): (5, 7), "01": (0, 4), "2": (8,)}


def lag_table(freqs, blocks):
    lags = 2 * freqs
    bins = np.arange(freqs)[:, None]
    shifts = np.arange(lags)[None, :] - lags // 2
    angle = np.mod(bins * shifts, lags) * (2.0 * math.pi / lags)
    both = np.stack([np.cos(angle), -np.sin(angle)]) / freqs
    both = both.reshape(2, blocks, freqs // blocks, lags).transpose(1, 0, 2, 3)
    return both.reshape(2 * freqs, lags).astype(jnp.bfloat16)


def one_hot(condition):
    return jnp.where(condition, 1.0, 0.0).astype(jnp.bfloat16)


def cell_rows(slot_cell, rank_table, own_g, share, blocks, cells):
    groups, slot_count = slot_cell.shape
    span = rank_table.shape[1]
    count = groups * share
    of_slot = lax.broadcasted_iota(jnp.int32, (slot_count, count), 0)
    incoming = lax.broadcasted_iota(jnp.int32, (slot_count, count), 1)
    pick = one_hot(of_slot == own_g * share + incoming % share)
    used = slot_cell >= 0
    high = jnp.where(used, slot_cell // span, -1).astype(jnp.float32).astype(jnp.bfloat16)
    low = jnp.where(used, slot_cell % span, 0).astype(jnp.float32).astype(jnp.bfloat16)
    group = lax.broadcasted_iota(jnp.int32, (groups, count), 0)
    mine = group == lax.broadcasted_iota(jnp.int32, (groups, count), 1) // share

    def own(values):
        spread = jnp.dot(values, pick, preferred_element_type=jnp.float32)
        return jnp.sum(jnp.where(mine, spread, 0.0), axis=0, keepdims=True)

    high, low = own(high), own(low)
    place = (rank_table % cells).astype(jnp.float32).astype(jnp.bfloat16)
    low_ids = lax.broadcasted_iota(jnp.int32, (span, count), 0).astype(jnp.float32)
    spread = jnp.dot(place, one_hot(low_ids == low), preferred_element_type=jnp.float32)
    high_ids = lax.broadcasted_iota(jnp.int32, (rank_table.shape[0], count), 0).astype(jnp.float32)
    place = jnp.sum(jnp.where(high_ids == high, spread, 0.0), axis=0, keepdims=True)
    owner = lax.broadcasted_iota(jnp.int32, (1, count), 1) % share // (share // blocks)
    return jnp.where(high >= 0, place + (owner * cells).astype(jnp.float32), -1.0)


def wait_for(ref, semaphore):
    pltpu.make_async_copy(ref, ref, semaphore).wait()


def kernel(sizes, spectra_hbm, pair_slot_hbm, slot_cell_hbm, rank_hbm, table_hbm, out_ref, spectra_ref, pair_slot_ref,
           slot_cell_ref, rank_ref, in_sems, mine, got, left, right, slots,
           opposite, total, matches, table, send_a, recv_a, send_b, recv_b, table_sem,
           x_send, x_recv, a_send, a_recv, b_send, b_recv):
    groups, blocks, rows, cells = sizes
    sensors = blocks * rows
    own_g, own_b = lax.axis_index("sensor"), lax.axis_index("partner")
    inputs = [
        pltpu.make_async_copy(source, to, in_sems.at[n])
        for n, (source, to) in enumerate((
            (spectra_hbm, spectra_ref), (pair_slot_hbm, pair_slot_ref), (slot_cell_hbm, slot_cell_ref), (rank_hbm, rank_ref)))
    ]
    for copy in inputs:
        copy.start()
    half = out_ref.shape[2] // blocks // 2

    partners = [lax.rem(own_b + step, blocks) for step in sorted(range(1, blocks), key=lambda n: abs(n - blocks // 2))]
    side = math.isqrt(groups)
    hops = sorted(range(1, groups), key=lambda n: abs(n // side - side // 2) + abs(n % side - side // 2))
    others_g = [
        lax.rem(own_g // side + n // side, side) * side + lax.rem(lax.rem(own_g, side) + n % side, side) for n in hops
    ]
    barrier = pltpu.get_barrier_semaphore()
    for to in partners:
        pl.semaphore_signal(barrier, inc=1, device_id=(own_g, to), device_id_type=MESH)
    for to in others_g:
        pl.semaphore_signal(barrier, inc=1, device_id=(to, own_b), device_id_type=MESH)
    table_copy = pltpu.make_async_copy(table_hbm, table, table_sem)
    table_copy.start()

    for copy in inputs:
        copy.wait()
    ids = pair_slot_ref[...].astype(jnp.float32).astype(jnp.bfloat16)
    first = lax.broadcasted_iota(jnp.int32, (rows, 2 * half), 1) < half
    for a in range(3):
        for pair in range(blocks // 2):
            lanes = slice(pair * 2 * half, (pair + 1) * 2 * half)
            real = spectra_ref[:, a, 0, lanes].astype(jnp.float32)
            imag = spectra_ref[:, a, 1, lanes].astype(jnp.float32)
            mine[2 * pair, a] = jnp.where(first, real, pltpu.roll(imag, half, 1)).astype(jnp.bfloat16)
            mine[2 * pair + 1, a] = jnp.where(first, pltpu.roll(real, half, 1), imag).astype(jnp.bfloat16)
    for b in range(blocks):
        mine[b, 3] = ids
    share = slot_cell_ref.shape[1] // groups
    at = cell_rows(slot_cell_ref[...], rank_ref[...], own_g, share, blocks, cells)
    row_ids = lax.broadcasted_iota(jnp.int32, (blocks * cells, groups * share), 0).astype(jnp.float32)
    matches[...] = one_hot(row_ids == at)
    pl.semaphore_wait(barrier, blocks + groups - 2)

    def bins_copy(to):
        return pltpu.make_async_remote_copy(
            src_ref=mine.at[to], dst_ref=got.at[own_b], send_sem=x_send, recv_sem=x_recv,
            device_id=(own_g, to), device_id_type=MESH)

    for to in partners:
        bins_copy(to).start()
    got[own_b] = mine[own_b]
    others = got.at[pl.ds(0, blocks - 1)]
    wait_for(others, x_recv)

    low = lax.broadcasted_iota(jnp.int32, (sensors, 2 * half), 1) < half
    wrap = right.shape[1] - sensors
    plain, swapped = [], []
    for a in range(3):
        x = got[:, a].reshape(sensors, 2 * half).astype(jnp.float32)
        plain.append(x)
        swapped.append(pltpu.roll(x, half, 1))

    def keep_right(n, x):
        x = x.astype(jnp.bfloat16)
        right[n, :sensors] = x
        right[n, sensors:] = x[:wrap]

    for a in range(3):
        x, y = plain[a], swapped[a]
        left[a] = x
        left[3 + a] = jnp.where(low, y, -y)
        if a > 0:
            left[5 + a] = jnp.where(low, x, -x)
            left[7 + a] = y
        keep_right(a, jnp.where(low, x, y))
        keep_right(3 + a, jnp.where(low, y, x))
    real = jnp.where(low, plain[0], swapped[1])
    imag = jnp.where(low, swapped[0], plain[1])
    left[10] = real
    left[11] = imag
    keep_right(6, real)
    keep_right(7, imag)

    window = sensors // 2
    table_of_slots = got[:, 3].reshape(sensors, sensors).astype(jnp.float32)
    lane = lax.broadcasted_iota(jnp.int32, (window, sensors), 1)
    pick = one_hot(lax.broadcasted_iota(jnp.int32, (sensors, rows * rows), 0)
                   == window + lax.broadcasted_iota(jnp.int32, (sensors, rows * rows), 1) % rows)
    keep = (lax.broadcasted_iota(jnp.int32, (window, rows * rows), 0) % rows
            == lax.broadcasted_iota(jnp.int32, (window, rows * rows), 1) // rows)
    for n, ordered in enumerate((table_of_slots, table_of_slots.T)):
        turned = jnp.concatenate([
            ordered[b * rows:(b + 1) * rows] if b == 0
            else pltpu.roll(ordered[b * rows:(b + 1) * rows], sensors - b * rows, 1) for b in range(blocks)], axis=0)
        joined = jnp.where(lane < window, turned[:window], pltpu.roll(turned[window:], window, 1))
        if n == 1:
            joined = jnp.where(lane % window < rows, -1.0, joined)
        slots[n] = joined
        spread = jnp.dot(turned[:window].astype(jnp.bfloat16), pick, preferred_element_type=jnp.float32)
        spread = jnp.where(keep, spread, 0.0)
        for b in range(blocks // 2):
            line = jnp.sum(spread[b * rows:(b + 1) * rows], axis=0, keepdims=True)
            for m in range(rows * rows // sensors):
                opposite[n, m, b:b + 1] = line[:, m * sensors:(m + 1) * sensors]

    slot_count = total.shape[1]
    slot_ids = lax.broadcasted_iota(jnp.int32, (slot_count, sensors), 0).astype(jnp.float32).astype(jnp.bfloat16)

    def select(row):
        row = jnp.broadcast_to(row, (16, sensors)).astype(jnp.bfloat16)
        row = jnp.concatenate([row] * (slot_count // 16), axis=0)
        return jnp.where(row == slot_ids, jnp.bfloat16(1), jnp.bfloat16(0))

    def slot_sums(k):
        chunk = CHUNKS[k]
        width = 2 * half * len(chunk)

        def factors(i, term, count):
            def wide(n):
                one = jnp.broadcast_to(left[n, pl.ds(i, 1), :], (16, 2 * half)).astype(jnp.bfloat16)
                return jnp.concatenate([one] * (count // 16), axis=0) if count > 16 else one

            if term == "01":
                return wide(10), wide(11)
            if term == "2":
                return wide(2), wide(5)
            a, b = term
            return wide(a), wide(3 + a), wide(5 + b), wide(7 + b)

        def products(i, at, count, term):
            of = factors(i, term, count)
            there = pl.ds(at, count)
            if term == "01":
                real, imag = right[6, there, :], right[7, there, :]
                return of[0] * real + of[1] * imag, of[1] * real - of[0] * imag
            if term == "2":
                both = of[0] * right[2, there, :] + of[1] * right[5, there, :]
                return both, both
            a, b = term
            one = of[0] * right[b, there, :] + of[1] * right[3 + b, there, :]
            two = of[2] * right[a, there, :] + of[3] * right[3 + a, there, :]
            return one + two, one - two

        def add(step, carried):
            start = pl.multiple_of(step * rows, rows)
            half_on = pl.multiple_of(step * rows + window, rows)
            added, taken = [], []
            pieces = [(start + u, start, window) for u in range(rows)], [(half_on + u, half_on, window) for u in range(rows)]
            order = [piece for both in zip(*pieces) for piece in both]
            order += [(start + u, half_on, rows) for u in range(rows)]
            for i, at, count in order:
                terms = [products(i, at, count, term) for term in chunk]
                added.append(jnp.concatenate([t[0] for t in terms], axis=1))
                taken.append(jnp.concatenate([t[1] for t in terms], axis=1))
            sums, differences = [], []
            for u in range(rows + rows * rows // sensors):
                if u < rows:
                    a, b = (select(slots[n, pl.ds(start + u, 1), :]) for n in range(2))
                else:
                    a, b = (select(opposite[n, u - rows, pl.ds(step, 1), :]) for n in range(2))
                sums.append(a + b)
                differences.append(a - b)
            for n, (chosen, values) in enumerate(((sums, added), (differences, taken))):
                total[n, :, :width] += jnp.dot(
                    jnp.concatenate(chosen, axis=1), jnp.concatenate(values, axis=0), preferred_element_type=jnp.float32)
            return carried

        total[:, :, :width] = jnp.zeros((2, slot_count, width), jnp.float32)
        lax.fori_loop(0, blocks // 2, add, 0)

    made = [tuple(c for term in chunk for c in MADE[term]) for chunk in CHUNKS]
    spans = []
    begin = 0
    for pairs in made:
        spans.append((begin, 2 * half * len(pairs)))
        begin += 2 * half * len(pairs)

    def sums_copy(k, to):
        start, width = spans[k]
        return pltpu.make_async_remote_copy(
            src_ref=send_a.at[pl.ds(pl.multiple_of(to * share, share), share), pl.ds(start, width)],
            dst_ref=recv_a.at[pl.ds(pl.multiple_of(own_g * share, share), share), pl.ds(start, width)],
            send_sem=a_send.at[k], recv_sem=a_recv.at[k],
            device_id=(to, own_b), device_id_type=MESH)

    def start_sums(k):
        start, width = spans[k]
        first = lax.broadcasted_iota(jnp.int32, (slot_count, 2 * half), 1) < half
        lines = []
        for m, term in enumerate(CHUNKS[k]):
            plus, minus = (total[n, :, 2 * half * m:2 * half * (m + 1)] for n in range(2))
            if term == "2":
                lines.append(jnp.where(first, plus, minus))
            elif term == "01":
                lines.append(jnp.where(first, plus, pltpu.roll(minus, half, 1)))
                lines.append(jnp.where(first, pltpu.roll(plus, half, 1), minus))
            else:
                lines.append(0.5 * (plus + minus))
                gap = 0.5 * (plus - minus)
                lines.append(jnp.where(first, gap, -gap))
        for m, line in enumerate(lines):
            at = start + 2 * half * m
            send_a[:, at:at + 2 * half] = line.astype(jnp.bfloat16)
        for to in others_g:
            sums_copy(k, to).start()
        own = pl.ds(pl.multiple_of(own_g * share, share), share)
        recv_a[own, start:start + width] = send_a[own, start:start + width]

    def cells_copy(k, to):
        start, width = spans[k]
        return pltpu.make_async_remote_copy(
            src_ref=send_b.at[to, :, pl.ds(start, width)],
            dst_ref=recv_b.at[own_b, :, pl.ds(start, width)],
            send_sem=b_send.at[k], recv_sem=b_recv.at[k],
            device_id=(own_g, to), device_id_type=MESH)

    def start_cells(k):
        start, width = spans[k]
        wait_for(recv_a.at[pl.ds(0, (groups - 1) * share), pl.ds(start, width)], a_recv.at[k])
        stacked = jnp.dot(matches[...], recv_a[:, start:start + width], preferred_element_type=jnp.float32)
        send_b[:, :, start:start + width] = stacked.astype(jnp.bfloat16).reshape(blocks, cells, width)
        for to in partners:
            cells_copy(k, to).start()
        recv_b[own_b, :, start:start + width] = send_b[own_b, :, start:start + width]

    def transform(k):
        start, width = spans[k]
        wait_for(recv_b.at[pl.ds(0, blocks - 1), :, pl.ds(start, width)], b_recv.at[k])
        lines = []
        for m in range(len(made[k])):
            at = start + 2 * half * m
            lines.append(jnp.concatenate([recv_b[b, :, at:at + 2 * half] for b in range(blocks)], axis=1))
        spectrum = jnp.concatenate(lines, axis=0) if len(lines) > 1 else lines[0]
        lag = jnp.dot(spectrum, table[...], preferred_element_type=jnp.float32).astype(jnp.bfloat16)
        for m, c in enumerate(made[k]):
            out_ref[c] = lag[m * cells:(m + 1) * cells]

    count = len(CHUNKS)
    for k in range(count):
        slot_sums(k)
        start_sums(k)
        if k >= 1:
            start_cells(k - 1)
    table_copy.wait()
    for k in range(count - 2):
        transform(k)
    wait_for(others, x_send)
    start_cells(count - 1)
    transform(count - 2)
    for k in range(count):
        start, width = spans[k]
        wait_for(send_a.at[pl.ds(0, (groups - 1) * share), pl.ds(start, width)], a_send.at[k])
        if k < count - 1:
            wait_for(send_b.at[pl.ds(0, blocks - 1), :, pl.ds(start, width)], b_send.at[k])
    transform(count - 1)
    start, width = spans[count - 1]
    wait_for(send_b.at[pl.ds(0, blocks - 1), :, pl.ds(start, width)], b_send.at[count - 1])


def on_device(spectra, pair_slot, slot_cell, cell_rank):
    rows, _, _, freqs = spectra.shape
    groups, slot_count = slot_cell.shape
    blocks = lax.axis_size("partner")
    sensors = rows * blocks
    cells = cell_rank.shape[0] // (groups * blocks)
    own_bins = 2 * freqs // blocks
    width = 9 * own_bins
    share = slot_count // groups

    table = jnp.asarray(lag_table(freqs, blocks))
    count = len(CHUNKS)
    widest = max(len(chunk) for chunk in CHUNKS) * own_bins
    vmem = pl.BlockSpec(memory_space=pltpu.VMEM)
    out = pl.pallas_call(
        functools.partial(kernel, (groups, blocks, rows, cells)),
        out_shape=pltpu.VMEM((9, cells, 2 * freqs), jnp.bfloat16),
        in_specs=[pl.BlockSpec(memory_space=pl.ANY)] * 5,
        out_specs=vmem,
        scratch_shapes=[
            pltpu.VMEM(spectra.shape, spectra.dtype),
            pltpu.VMEM(pair_slot.shape, pair_slot.dtype),
            pltpu.VMEM(slot_cell.shape, slot_cell.dtype),
            pltpu.VMEM((cell_rank.shape[0] // 128, 128), cell_rank.dtype),
            pltpu.SemaphoreType.DMA((4,)),
            pltpu.VMEM((blocks, 4, rows, own_bins), jnp.bfloat16),
            pltpu.VMEM((blocks, 4, rows, own_bins), jnp.bfloat16),
            pltpu.VMEM((12, sensors, own_bins), jnp.float32),
            pltpu.VMEM((8, sensors + sensors // 2, own_bins), jnp.bfloat16),
            pltpu.VMEM((2, sensors // 2, sensors), jnp.float32),
            pltpu.VMEM((2, rows * rows // sensors, blocks, sensors), jnp.float32),
            pltpu.VMEM((2, slot_count, widest), jnp.float32),
            pltpu.VMEM((blocks * cells, groups * share), jnp.bfloat16),
            pltpu.VMEM((2 * freqs, 2 * freqs), jnp.bfloat16),
            pltpu.VMEM((slot_count, width), jnp.bfloat16),
            pltpu.VMEM((groups * share, width), jnp.bfloat16),
            pltpu.VMEM((blocks, cells, width), jnp.bfloat16),
            pltpu.VMEM((blocks, cells, width), jnp.bfloat16),
            pltpu.SemaphoreType.DMA,
            pltpu.SemaphoreType.DMA,
            pltpu.SemaphoreType.DMA,
            pltpu.SemaphoreType.DMA((count,)),
            pltpu.SemaphoreType.DMA((count,)),
            pltpu.SemaphoreType.DMA((count,)),
            pltpu.SemaphoreType.DMA((count,)),
        ],
        compiler_params=pltpu.CompilerParams(
            collective_id=0, has_side_effects=True, vmem_limit_bytes=56 * 2**20),
        name="stack_pairs",
    )(spectra, pair_slot, slot_cell, cell_rank.reshape(-1, 128), table)
    return out.transpose(1, 0, 2)


def solution(mesh):
    in_specs = (
        P(("sensor", "partner"), None, None, None),
        P(("sensor", "partner"), None),
        P(),
        P(),
    )
    out_specs = P(("sensor", "partner"), None, None)
    return jax.shard_map(
        on_device, mesh=mesh, in_specs=in_specs, out_specs=out_specs, check_vma=False
    )
```

```python
import functools
import math

import jax
import jax.numpy as jnp
import numpy as np
from jax import lax
from jax.experimental import pallas as pl
from jax.experimental.pallas import tpu as pltpu
from jax.sharding import PartitionSpec as P

MESH = pl.DeviceIdType.MESH
CHUNKS = (((0, 1), (0, 2)), ((1, 2), "01"), ("2",))
MADE = {(0, 1): (1, 3), (0, 2): (2, 6), (1, 2): (5, 7), "01": (0, 4), "2": (8,)}


def lag_table(freqs, blocks):
    lags = 2 * freqs
    bins = np.arange(freqs)[:, None]
    shifts = np.arange(lags)[None, :] - lags // 2
    angle = np.mod(bins * shifts, lags) * (2.0 * math.pi / lags)
    both = np.stack([np.cos(angle), -np.sin(angle)]) / freqs
    both = both.reshape(2, blocks, freqs // blocks, lags).transpose(1, 0, 2, 3)
    return both.reshape(2 * freqs, lags).astype(jnp.bfloat16)


def one_hot(condition):
    return jnp.where(condition, 1.0, 0.0).astype(jnp.bfloat16)


def cell_rows(slot_cell, rank_table, own_g, share, blocks, cells):
    groups, slot_count = slot_cell.shape
    span = rank_table.shape[1]
    count = groups * share
    of_slot = lax.broadcasted_iota(jnp.int32, (slot_count, count), 0)
    incoming = lax.broadcasted_iota(jnp.int32, (slot_count, count), 1)
    pick = one_hot(of_slot == own_g * share + incoming % share)
    used = slot_cell >= 0
    high = jnp.where(used, slot_cell // span, -1).astype(jnp.float32).astype(jnp.bfloat16)
    low = jnp.where(used, slot_cell % span, 0).astype(jnp.float32).astype(jnp.bfloat16)
    group = lax.broadcasted_iota(jnp.int32, (groups, count), 0)
    mine = group == lax.broadcasted_iota(jnp.int32, (groups, count), 1) // share

    def own(values):
        spread = jnp.dot(values, pick, preferred_element_type=jnp.float32)
        return jnp.sum(jnp.where(mine, spread, 0.0), axis=0, keepdims=True)

    high, low = own(high), own(low)
    place = (rank_table % cells).astype(jnp.float32).astype(jnp.bfloat16)
    low_ids = lax.broadcasted_iota(jnp.int32, (span, count), 0).astype(jnp.float32)
    spread = jnp.dot(place, one_hot(low_ids == low), preferred_element_type=jnp.float32)
    high_ids = lax.broadcasted_iota(jnp.int32, (rank_table.shape[0], count), 0).astype(jnp.float32)
    place = jnp.sum(jnp.where(high_ids == high, spread, 0.0), axis=0, keepdims=True)
    owner = lax.broadcasted_iota(jnp.int32, (1, count), 1) % share // (share // blocks)
    return jnp.where(high >= 0, place + (owner * cells).astype(jnp.float32), -1.0)


def wait_for(ref, semaphore):
    pltpu.make_async_copy(ref, ref, semaphore).wait()


def kernel(sizes, spectra_hbm, pair_slot_hbm, slot_cell_hbm, rank_hbm, table_hbm, out_ref, spectra_ref, pair_slot_ref,
           slot_cell_ref, rank_ref, in_sems, mine, got, left, right, slots,
           opposite, total, matches, table, send_a, recv_a, send_b, recv_b, table_sem,
           x_send, x_recv, a_send, a_recv, b_send, b_recv):
    groups, blocks, rows, cells = sizes
    sensors = blocks * rows
    own_g, own_b = lax.axis_index("sensor"), lax.axis_index("partner")
    inputs = [
        pltpu.make_async_copy(source, to, in_sems.at[n])
        for n, (source, to) in enumerate((
            (spectra_hbm, spectra_ref), (pair_slot_hbm, pair_slot_ref), (slot_cell_hbm, slot_cell_ref), (rank_hbm, rank_ref)))
    ]
    for copy in inputs:
        copy.start()
    half = out_ref.shape[2] // blocks // 2

    partners = [lax.rem(own_b + step, blocks) for step in sorted(range(1, blocks), key=lambda n: abs(n - blocks // 2))]
    side = math.isqrt(groups)
    hops = sorted(range(1, groups), key=lambda n: abs(n // side - side // 2) + abs(n % side - side // 2))
    others_g = [
        lax.rem(own_g // side + n // side, side) * side + lax.rem(lax.rem(own_g, side) + n % side, side) for n in hops
    ]
    barrier = pltpu.get_barrier_semaphore()
    for to in partners:
        pl.semaphore_signal(barrier, inc=1, device_id=(own_g, to), device_id_type=MESH)
    for to in others_g:
        pl.semaphore_signal(barrier, inc=1, device_id=(to, own_b), device_id_type=MESH)
    table_copy = pltpu.make_async_copy(table_hbm, table, table_sem)
    table_copy.start()

    for copy in inputs:
        copy.wait()
    ids = pair_slot_ref[...].astype(jnp.float32).astype(jnp.bfloat16)
    first = lax.broadcasted_iota(jnp.int32, (rows, 2 * half), 1) < half
    for a in range(3):
        for pair in range(blocks // 2):
            lanes = slice(pair * 2 * half, (pair + 1) * 2 * half)
            real = spectra_ref[:, a, 0, lanes].astype(jnp.float32)
            imag = spectra_ref[:, a, 1, lanes].astype(jnp.float32)
            mine[2 * pair, a] = jnp.where(first, real, pltpu.roll(imag, half, 1)).astype(jnp.bfloat16)
            mine[2 * pair + 1, a] = jnp.where(first, pltpu.roll(real, half, 1), imag).astype(jnp.bfloat16)
    for b in range(blocks):
        mine[b, 3] = ids
    share = slot_cell_ref.shape[1] // groups
    at = cell_rows(slot_cell_ref[...], rank_ref[...], own_g, share, blocks, cells)
    row_ids = lax.broadcasted_iota(jnp.int32, (blocks * cells, groups * share), 0).astype(jnp.float32)
    matches[...] = one_hot(row_ids == at)
    pl.semaphore_wait(barrier, blocks + groups - 2)

    def bins_copy(to):
        return pltpu.make_async_remote_copy(
            src_ref=mine.at[to], dst_ref=got.at[own_b], send_sem=x_send, recv_sem=x_recv,
            device_id=(own_g, to), device_id_type=MESH)

    for to in partners:
        bins_copy(to).start()
    got[own_b] = mine[own_b]
    others = got.at[pl.ds(0, blocks - 1)]
    wait_for(others, x_recv)

    low = lax.broadcasted_iota(jnp.int32, (sensors, 2 * half), 1) < half
    wrap = right.shape[1] - sensors
    plain, swapped = [], []
    for a in range(3):
        x = got[:, a].reshape(sensors, 2 * half).astype(jnp.float32)
        plain.append(x)
        swapped.append(pltpu.roll(x, half, 1))

    def keep_right(n, x):
        x = x.astype(jnp.bfloat16)
        right[n, :sensors] = x
        right[n, sensors:] = x[:wrap]

    for a in range(3):
        x, y = plain[a], swapped[a]
        left[a] = x
        left[3 + a] = jnp.where(low, y, -y)
        if a > 0:
            left[5 + a] = jnp.where(low, x, -x)
            left[7 + a] = y
        keep_right(a, jnp.where(low, x, y))
        keep_right(3 + a, jnp.where(low, y, x))
    real = jnp.where(low, plain[0], swapped[1])
    imag = jnp.where(low, swapped[0], plain[1])
    left[10] = real
    left[11] = imag
    keep_right(6, real)
    keep_right(7, imag)

    window = sensors // 2
    table_of_slots = got[:, 3].reshape(sensors, sensors).astype(jnp.float32)
    lane = lax.broadcasted_iota(jnp.int32, (window, sensors), 1)
    pick = one_hot(lax.broadcasted_iota(jnp.int32, (sensors, rows * rows), 0)
                   == window + lax.broadcasted_iota(jnp.int32, (sensors, rows * rows), 1) % rows)
    keep = (lax.broadcasted_iota(jnp.int32, (window, rows * rows), 0) % rows
            == lax.broadcasted_iota(jnp.int32, (window, rows * rows), 1) // rows)
    for n, ordered in enumerate((table_of_slots, table_of_slots.T)):
        turned = jnp.concatenate([
            ordered[b * rows:(b + 1) * rows] if b == 0
            else pltpu.roll(ordered[b * rows:(b + 1) * rows], sensors - b * rows, 1) for b in range(blocks)], axis=0)
        joined = jnp.where(lane < window, turned[:window], pltpu.roll(turned[window:], window, 1))
        if n == 1:
            joined = jnp.where(lane % window < rows, -1.0, joined)
        slots[n] = joined
        spread = jnp.dot(turned[:window].astype(jnp.bfloat16), pick, preferred_element_type=jnp.float32)
        spread = jnp.where(keep, spread, 0.0)
        for b in range(blocks // 2):
            line = jnp.sum(spread[b * rows:(b + 1) * rows], axis=0, keepdims=True)
            for m in range(rows * rows // sensors):
                opposite[n, m, b:b + 1] = line[:, m * sensors:(m + 1) * sensors]

    slot_count = total.shape[1]
    slot_ids = lax.broadcasted_iota(jnp.int32, (slot_count, sensors), 0).astype(jnp.float32).astype(jnp.bfloat16)

    def select(row):
        row = jnp.broadcast_to(row, (16, sensors)).astype(jnp.bfloat16)
        row = jnp.concatenate([row] * (slot_count // 16), axis=0)
        return jnp.where(row == slot_ids, jnp.bfloat16(1), jnp.bfloat16(0))

    def slot_sums(k):
        chunk = CHUNKS[k]
        width = 2 * half * len(chunk)

        def factors(i, term, count):
            def wide(n):
                one = jnp.broadcast_to(left[n, pl.ds(i, 1), :], (16, 2 * half)).astype(jnp.bfloat16)
                return jnp.concatenate([one] * (count // 16), axis=0) if count > 16 else one

            if term == "01":
                return wide(10), wide(11)
            if term == "2":
                return wide(2), wide(5)
            a, b = term
            return wide(a), wide(3 + a), wide(5 + b), wide(7 + b)

        def products(i, at, count, term):
            of = factors(i, term, count)
            there = pl.ds(at, count)
            if term == "01":
                real, imag = right[6, there, :], right[7, there, :]
                return of[0] * real + of[1] * imag, of[1] * real - of[0] * imag
            if term == "2":
                both = of[0] * right[2, there, :] + of[1] * right[5, there, :]
                return both, both
            a, b = term
            one = of[0] * right[b, there, :] + of[1] * right[3 + b, there, :]
            two = of[2] * right[a, there, :] + of[3] * right[3 + a, there, :]
            return one + two, one - two

        def add(step, carried):
            start = pl.multiple_of(step * rows, rows)
            half_on = pl.multiple_of(step * rows + window, rows)
            added, taken = [], []
            pieces = [(start + u, start, window) for u in range(rows)], [(half_on + u, half_on, window) for u in range(rows)]
            order = [piece for both in zip(*pieces) for piece in both]
            order += [(start + u, half_on, rows) for u in range(rows)]
            for i, at, count in order:
                terms = [products(i, at, count, term) for term in chunk]
                added.append(jnp.concatenate([t[0] for t in terms], axis=1))
                taken.append(jnp.concatenate([t[1] for t in terms], axis=1))
            sums, differences = [], []
            for u in range(rows + rows * rows // sensors):
                if u < rows:
                    a, b = (select(slots[n, pl.ds(start + u, 1), :]) for n in range(2))
                else:
                    a, b = (select(opposite[n, u - rows, pl.ds(step, 1), :]) for n in range(2))
                sums.append(a + b)
                differences.append(a - b)
            for n, (chosen, values) in enumerate(((sums, added), (differences, taken))):
                total[n, :, :width] += jnp.dot(
                    jnp.concatenate(chosen, axis=1), jnp.concatenate(values, axis=0), preferred_element_type=jnp.float32)
            return carried

        total[:, :, :width] = jnp.zeros((2, slot_count, width), jnp.float32)
        lax.fori_loop(0, blocks // 2, add, 0)

    made = [tuple(c for term in chunk for c in MADE[term]) for chunk in CHUNKS]
    spans = []
    begin = 0
    for pairs in made:
        spans.append((begin, 2 * half * len(pairs)))
        begin += 2 * half * len(pairs)

    def sums_copy(k, to):
        start, width = spans[k]
        return pltpu.make_async_remote_copy(
            src_ref=send_a.at[pl.ds(pl.multiple_of(to * share, share), share), pl.ds(start, width)],
            dst_ref=recv_a.at[pl.ds(pl.multiple_of(own_g * share, share), share), pl.ds(start, width)],
            send_sem=a_send.at[k], recv_sem=a_recv.at[k],
            device_id=(to, own_b), device_id_type=MESH)

    def start_sums(k):
        start, width = spans[k]
        first = lax.broadcasted_iota(jnp.int32, (slot_count, 2 * half), 1) < half
        lines = []
        for m, term in enumerate(CHUNKS[k]):
            plus, minus = (total[n, :, 2 * half * m:2 * half * (m + 1)] for n in range(2))
            if term == "2":
                lines.append(jnp.where(first, plus, minus))
            elif term == "01":
                lines.append(jnp.where(first, plus, pltpu.roll(minus, half, 1)))
                lines.append(jnp.where(first, pltpu.roll(plus, half, 1), minus))
            else:
                lines.append(0.5 * (plus + minus))
                gap = 0.5 * (plus - minus)
                lines.append(jnp.where(first, gap, -gap))
        for m, line in enumerate(lines):
            at = start + 2 * half * m
            send_a[:, at:at + 2 * half] = line.astype(jnp.bfloat16)
        for to in others_g:
            sums_copy(k, to).start()
        own = pl.ds(pl.multiple_of(own_g * share, share), share)
        recv_a[own, start:start + width] = send_a[own, start:start + width]

    def cells_copy(k, to):
        start, width = spans[k]
        return pltpu.make_async_remote_copy(
            src_ref=send_b.at[to, :, pl.ds(start, width)],
            dst_ref=recv_b.at[own_b, :, pl.ds(start, width)],
            send_sem=b_send.at[k], recv_sem=b_recv.at[k],
            device_id=(own_g, to), device_id_type=MESH)

    def start_cells(k):
        start, width = spans[k]
        wait_for(recv_a.at[pl.ds(0, (groups - 1) * share), pl.ds(start, width)], a_recv.at[k])
        stacked = jnp.dot(matches[...], recv_a[:, start:start + width], preferred_element_type=jnp.float32)
        send_b[:, :, start:start + width] = stacked.astype(jnp.bfloat16).reshape(blocks, cells, width)
        for to in partners:
            cells_copy(k, to).start()
        recv_b[own_b, :, start:start + width] = send_b[own_b, :, start:start + width]

    def transform(k):
        start, width = spans[k]
        wait_for(recv_b.at[pl.ds(0, blocks - 1), :, pl.ds(start, width)], b_recv.at[k])
        lines = []
        for m in range(len(made[k])):
            at = start + 2 * half * m
            lines.append(jnp.concatenate([recv_b[b, :, at:at + 2 * half] for b in range(blocks)], axis=1))
        spectrum = jnp.concatenate(lines, axis=0) if len(lines) > 1 else lines[0]
        lag = jnp.dot(spectrum, table[...], preferred_element_type=jnp.float32).astype(jnp.bfloat16)
        for m, c in enumerate(made[k]):
            out_ref[c] = lag[m * cells:(m + 1) * cells]

    count = len(CHUNKS)
    for k in range(count):
        slot_sums(k)
        start_sums(k)
    table_copy.wait()
    wait_for(others, x_send)
    for k in range(count):
        start_cells(k)
    for k in range(count - 1):
        transform(k)
    for k in range(count):
        start, width = spans[k]
        wait_for(send_a.at[pl.ds(0, (groups - 1) * share), pl.ds(start, width)], a_send.at[k])
        if k < count - 1:
            wait_for(send_b.at[pl.ds(0, blocks - 1), :, pl.ds(start, width)], b_send.at[k])
    transform(count - 1)
    start, width = spans[count - 1]
    wait_for(send_b.at[pl.ds(0, blocks - 1), :, pl.ds(start, width)], b_send.at[count - 1])


def on_device(spectra, pair_slot, slot_cell, cell_rank):
    rows, _, _, freqs = spectra.shape
    groups, slot_count = slot_cell.shape
    blocks = lax.axis_size("partner")
    sensors = rows * blocks
    cells = cell_rank.shape[0] // (groups * blocks)
    own_bins = 2 * freqs // blocks
    width = 9 * own_bins
    share = slot_count // groups

    table = jnp.asarray(lag_table(freqs, blocks))
    count = len(CHUNKS)
    widest = max(len(chunk) for chunk in CHUNKS) * own_bins
    vmem = pl.BlockSpec(memory_space=pltpu.VMEM)
    out = pl.pallas_call(
        functools.partial(kernel, (groups, blocks, rows, cells)),
        out_shape=pltpu.VMEM((9, cells, 2 * freqs), jnp.bfloat16),
        in_specs=[pl.BlockSpec(memory_space=pl.ANY)] * 5,
        out_specs=vmem,
        scratch_shapes=[
            pltpu.VMEM(spectra.shape, spectra.dtype),
            pltpu.VMEM(pair_slot.shape, pair_slot.dtype),
            pltpu.VMEM(slot_cell.shape, slot_cell.dtype),
            pltpu.VMEM((cell_rank.shape[0] // 128, 128), cell_rank.dtype),
            pltpu.SemaphoreType.DMA((4,)),
            pltpu.VMEM((blocks, 4, rows, own_bins), jnp.bfloat16),
            pltpu.VMEM((blocks, 4, rows, own_bins), jnp.bfloat16),
            pltpu.VMEM((12, sensors, own_bins), jnp.float32),
            pltpu.VMEM((8, sensors + sensors // 2, own_bins), jnp.bfloat16),
            pltpu.VMEM((2, sensors // 2, sensors), jnp.float32),
            pltpu.VMEM((2, rows * rows // sensors, blocks, sensors), jnp.float32),
            pltpu.VMEM((2, slot_count, widest), jnp.float32),
            pltpu.VMEM((blocks * cells, groups * share), jnp.bfloat16),
            pltpu.VMEM((2 * freqs, 2 * freqs), jnp.bfloat16),
            pltpu.VMEM((slot_count, width), jnp.bfloat16),
            pltpu.VMEM((groups * share, width), jnp.bfloat16),
            pltpu.VMEM((blocks, cells, width), jnp.bfloat16),
            pltpu.VMEM((blocks, cells, width), jnp.bfloat16),
            pltpu.SemaphoreType.DMA,
            pltpu.SemaphoreType.DMA,
            pltpu.SemaphoreType.DMA,
            pltpu.SemaphoreType.DMA((count,)),
            pltpu.SemaphoreType.DMA((count,)),
            pltpu.SemaphoreType.DMA((count,)),
            pltpu.SemaphoreType.DMA((count,)),
        ],
        compiler_params=pltpu.CompilerParams(
            collective_id=0, has_side_effects=True, vmem_limit_bytes=56 * 2**20),
        name="stack_pairs",
    )(spectra, pair_slot, slot_cell, cell_rank.reshape(-1, 128), table)
    return out.transpose(1, 0, 2)


def solution(mesh):
    in_specs = (
        P(("sensor", "partner"), None, None, None),
        P(("sensor", "partner"), None),
        P(),
        P(),
    )
    out_specs = P(("sensor", "partner"), None, None)
    return jax.shard_map(
        on_device, mesh=mesh, in_specs=in_specs, out_specs=out_specs, check_vma=False
    )
```

```python
import functools
import math

import jax
import jax.numpy as jnp
import numpy as np
from jax import lax
from jax.experimental import pallas as pl
from jax.experimental.pallas import tpu as pltpu
from jax.sharding import PartitionSpec as P

MESH = pl.DeviceIdType.MESH
CHUNKS = (((0, 1), (0, 2)), ((1, 2), "01"), ("2",))
MADE = {(0, 1): (1, 3), (0, 2): (2, 6), (1, 2): (5, 7), "01": (0, 4), "2": (8,)}


def lag_table(freqs, blocks):
    lags = 2 * freqs
    bins = np.arange(freqs)[:, None]
    shifts = np.arange(lags)[None, :] - lags // 2
    angle = np.mod(bins * shifts, lags) * (2.0 * math.pi / lags)
    both = np.stack([np.cos(angle), -np.sin(angle)]) / freqs
    both = both.reshape(2, blocks, freqs // blocks, lags).transpose(1, 0, 2, 3)
    return both.reshape(2 * freqs, lags).astype(jnp.bfloat16)


def one_hot(condition):
    return jnp.where(condition, 1.0, 0.0).astype(jnp.bfloat16)


def cell_rows(slot_cell, rank_table, own_g, share, blocks, cells):
    groups, slot_count = slot_cell.shape
    span = rank_table.shape[1]
    count = groups * share
    of_slot = lax.broadcasted_iota(jnp.int32, (slot_count, count), 0)
    incoming = lax.broadcasted_iota(jnp.int32, (slot_count, count), 1)
    pick = one_hot(of_slot == own_g * share + incoming % share)
    used = slot_cell >= 0
    high = jnp.where(used, slot_cell // span, -1).astype(jnp.float32).astype(jnp.bfloat16)
    low = jnp.where(used, slot_cell % span, 0).astype(jnp.float32).astype(jnp.bfloat16)
    group = lax.broadcasted_iota(jnp.int32, (groups, count), 0)
    mine = group == lax.broadcasted_iota(jnp.int32, (groups, count), 1) // share

    def own(values):
        spread = jnp.dot(values, pick, preferred_element_type=jnp.float32)
        return jnp.sum(jnp.where(mine, spread, 0.0), axis=0, keepdims=True)

    high, low = own(high), own(low)
    place = (rank_table % cells).astype(jnp.float32).astype(jnp.bfloat16)
    low_ids = lax.broadcasted_iota(jnp.int32, (span, count), 0).astype(jnp.float32)
    spread = jnp.dot(place, one_hot(low_ids == low), preferred_element_type=jnp.float32)
    high_ids = lax.broadcasted_iota(jnp.int32, (rank_table.shape[0], count), 0).astype(jnp.float32)
    place = jnp.sum(jnp.where(high_ids == high, spread, 0.0), axis=0, keepdims=True)
    owner = lax.broadcasted_iota(jnp.int32, (1, count), 1) % share // (share // blocks)
    return jnp.where(high >= 0, place + (owner * cells).astype(jnp.float32), -1.0)


def wait_for(ref, semaphore):
    pltpu.make_async_copy(ref, ref, semaphore).wait()


def kernel(sizes, spectra_hbm, pair_slot_hbm, slot_cell_hbm, rank_hbm, table_hbm, out_ref, spectra_ref, pair_slot_ref,
           slot_cell_ref, rank_ref, in_sems, mine, got, left, right, slots,
           opposite, total, matches, table, send_a, recv_a, send_b, recv_b, table_sem,
           x_send, x_recv, a_send, a_recv, b_send, b_recv):
    groups, blocks, rows, cells = sizes
    sensors = blocks * rows
    own_g, own_b = lax.axis_index("sensor"), lax.axis_index("partner")
    inputs = [
        pltpu.make_async_copy(source, to, in_sems.at[n])
        for n, (source, to) in enumerate((
            (spectra_hbm, spectra_ref), (pair_slot_hbm, pair_slot_ref), (slot_cell_hbm, slot_cell_ref), (rank_hbm, rank_ref)))
    ]
    for copy in inputs:
        copy.start()
    half = out_ref.shape[2] // blocks // 2

    partners = [lax.rem(own_b + step, blocks) for step in sorted(range(1, blocks), key=lambda n: abs(n - blocks // 2))]
    side = math.isqrt(groups)
    hops = sorted(range(1, groups), key=lambda n: abs(n // side - side // 2) + abs(n % side - side // 2))
    others_g = [
        lax.rem(own_g // side + n // side, side) * side + lax.rem(lax.rem(own_g, side) + n % side, side) for n in hops
    ]
    barrier = pltpu.get_barrier_semaphore()
    for to in partners:
        pl.semaphore_signal(barrier, inc=1, device_id=(own_g, to), device_id_type=MESH)
    for to in others_g:
        pl.semaphore_signal(barrier, inc=1, device_id=(to, own_b), device_id_type=MESH)
    table_copy = pltpu.make_async_copy(table_hbm, table, table_sem)
    table_copy.start()

    for copy in inputs:
        copy.wait()
    ids = pair_slot_ref[...].astype(jnp.float32).astype(jnp.bfloat16)
    first = lax.broadcasted_iota(jnp.int32, (rows, 2 * half), 1) < half
    for a in range(3):
        for pair in range(blocks // 2):
            lanes = slice(pair * 2 * half, (pair + 1) * 2 * half)
            real = spectra_ref[:, a, 0, lanes].astype(jnp.float32)
            imag = spectra_ref[:, a, 1, lanes].astype(jnp.float32)
            mine[2 * pair, a] = jnp.where(first, real, pltpu.roll(imag, half, 1)).astype(jnp.bfloat16)
            mine[2 * pair + 1, a] = jnp.where(first, pltpu.roll(real, half, 1), imag).astype(jnp.bfloat16)
    for b in range(blocks):
        mine[b, 3] = ids
    share = slot_cell_ref.shape[1] // groups
    at = cell_rows(slot_cell_ref[...], rank_ref[...], own_g, share, blocks, cells)
    row_ids = lax.broadcasted_iota(jnp.int32, (blocks * cells, groups * share), 0).astype(jnp.float32)
    matches[...] = one_hot(row_ids == at)
    pl.semaphore_wait(barrier, blocks + groups - 2)

    def bins_copy(to):
        return pltpu.make_async_remote_copy(
            src_ref=mine.at[to], dst_ref=got.at[own_b], send_sem=x_send, recv_sem=x_recv,
            device_id=(own_g, to), device_id_type=MESH)

    for to in partners:
        bins_copy(to).start()
    got[own_b] = mine[own_b]
    others = got.at[pl.ds(0, blocks - 1)]
    wait_for(others, x_recv)

    low = lax.broadcasted_iota(jnp.int32, (sensors, 2 * half), 1) < half
    wrap = right.shape[1] - sensors
    plain, swapped = [], []
    for a in range(3):
        x = got[:, a].reshape(sensors, 2 * half).astype(jnp.float32)
        plain.append(x)
        swapped.append(pltpu.roll(x, half, 1))

    def keep_right(n, x):
        x = x.astype(jnp.bfloat16)
        right[n, :sensors] = x
        right[n, sensors:] = x[:wrap]

    for a in range(3):
        x, y = plain[a], swapped[a]
        left[a] = x
        left[3 + a] = jnp.where(low, y, -y)
        if a > 0:
            left[5 + a] = jnp.where(low, x, -x)
            left[7 + a] = y
        keep_right(a, jnp.where(low, x, y))
        keep_right(3 + a, jnp.where(low, y, x))
    real = jnp.where(low, plain[0], swapped[1])
    imag = jnp.where(low, swapped[0], plain[1])
    left[10] = real
    left[11] = imag
    keep_right(6, real)
    keep_right(7, imag)

    window = sensors // 2
    table_of_slots = got[:, 3].reshape(sensors, sensors).astype(jnp.float32)
    lane = lax.broadcasted_iota(jnp.int32, (window, sensors), 1)
    pick = one_hot(lax.broadcasted_iota(jnp.int32, (sensors, rows * rows), 0)
                   == window + lax.broadcasted_iota(jnp.int32, (sensors, rows * rows), 1) % rows)
    keep = (lax.broadcasted_iota(jnp.int32, (window, rows * rows), 0) % rows
            == lax.broadcasted_iota(jnp.int32, (window, rows * rows), 1) // rows)
    for n, ordered in enumerate((table_of_slots, table_of_slots.T)):
        turned = jnp.concatenate([
            ordered[b * rows:(b + 1) * rows] if b == 0
            else pltpu.roll(ordered[b * rows:(b + 1) * rows], sensors - b * rows, 1) for b in range(blocks)], axis=0)
        joined = jnp.where(lane < window, turned[:window], pltpu.roll(turned[window:], window, 1))
        if n == 1:
            joined = jnp.where(lane % window < rows, -1.0, joined)
        slots[n] = joined
        spread = jnp.dot(turned[:window].astype(jnp.bfloat16), pick, preferred_element_type=jnp.float32)
        spread = jnp.where(keep, spread, 0.0)
        for b in range(blocks // 2):
            line = jnp.sum(spread[b * rows:(b + 1) * rows], axis=0, keepdims=True)
            for m in range(rows * rows // sensors):
                opposite[n, m, b:b + 1] = line[:, m * sensors:(m + 1) * sensors]

    slot_count = total.shape[1]
    slot_ids = lax.broadcasted_iota(jnp.int32, (slot_count, sensors), 0).astype(jnp.float32).astype(jnp.bfloat16)

    def select(row):
        row = jnp.broadcast_to(row, (16, sensors)).astype(jnp.bfloat16)
        row = jnp.concatenate([row] * (slot_count // 16), axis=0)
        return jnp.where(row == slot_ids, jnp.bfloat16(1), jnp.bfloat16(0))

    def slot_sums(k):
        chunk = CHUNKS[k]
        width = 2 * half * len(chunk)

        def factors(i, term, count):
            def wide(n):
                one = jnp.broadcast_to(left[n, pl.ds(i, 1), :], (16, 2 * half)).astype(jnp.bfloat16)
                return jnp.concatenate([one] * (count // 16), axis=0) if count > 16 else one

            if term == "01":
                return wide(10), wide(11)
            if term == "2":
                return wide(2), wide(5)
            a, b = term
            return wide(a), wide(3 + a), wide(5 + b), wide(7 + b)

        def products(i, at, count, term):
            of = factors(i, term, count)
            there = pl.ds(at, count)
            if term == "01":
                real, imag = right[6, there, :], right[7, there, :]
                return of[0] * real + of[1] * imag, of[1] * real - of[0] * imag
            if term == "2":
                both = of[0] * right[2, there, :] + of[1] * right[5, there, :]
                return both, both
            a, b = term
            one = of[0] * right[b, there, :] + of[1] * right[3 + b, there, :]
            two = of[2] * right[a, there, :] + of[3] * right[3 + a, there, :]
            return one + two, one - two

        def add(step, carried):
            start = pl.multiple_of(step * rows, rows)
            half_on = pl.multiple_of(step * rows + window, rows)
            added, taken = [], []
            pieces = [(start + u, start, window) for u in range(rows)], [(half_on + u, half_on, window) for u in range(rows)]
            order = [piece for both in zip(*pieces) for piece in both]
            order += [(start + u, half_on, rows) for u in range(rows)]
            for i, at, count in order:
                terms = [products(i, at, count, term) for term in chunk]
                added.append(jnp.concatenate([t[0] for t in terms], axis=1))
                taken.append(jnp.concatenate([t[1] for t in terms], axis=1))
            sums, differences = [], []
            for u in range(rows + rows * rows // sensors):
                if u < rows:
                    a, b = (select(slots[n, pl.ds(start + u, 1), :]) for n in range(2))
                else:
                    a, b = (select(opposite[n, u - rows, pl.ds(step, 1), :]) for n in range(2))
                sums.append(a + b)
                differences.append(a - b)
            for n, (chosen, values) in enumerate(((sums, added), (differences, taken))):
                total[n, :, :width] += jnp.dot(
                    jnp.concatenate(chosen, axis=1), jnp.concatenate(values, axis=0), preferred_element_type=jnp.float32)
            return carried

        total[:, :, :width] = jnp.zeros((2, slot_count, width), jnp.float32)
        lax.fori_loop(0, blocks // 2, add, 0, unroll=4)

    made = [tuple(c for term in chunk for c in MADE[term]) for chunk in CHUNKS]
    spans = []
    begin = 0
    for pairs in made:
        spans.append((begin, 2 * half * len(pairs)))
        begin += 2 * half * len(pairs)

    def sums_copy(k, to):
        start, width = spans[k]
        return pltpu.make_async_remote_copy(
            src_ref=send_a.at[pl.ds(pl.multiple_of(to * share, share), share), pl.ds(start, width)],
            dst_ref=recv_a.at[pl.ds(pl.multiple_of(own_g * share, share), share), pl.ds(start, width)],
            send_sem=a_send.at[k], recv_sem=a_recv.at[k],
            device_id=(to, own_b), device_id_type=MESH)

    def start_sums(k):
        start, width = spans[k]
        first = lax.broadcasted_iota(jnp.int32, (slot_count, 2 * half), 1) < half
        lines = []
        for m, term in enumerate(CHUNKS[k]):
            plus, minus = (total[n, :, 2 * half * m:2 * half * (m + 1)] for n in range(2))
            if term == "2":
                lines.append(jnp.where(first, plus, minus))
            elif term == "01":
                lines.append(jnp.where(first, plus, pltpu.roll(minus, half, 1)))
                lines.append(jnp.where(first, pltpu.roll(plus, half, 1), minus))
            else:
                lines.append(0.5 * (plus + minus))
                gap = 0.5 * (plus - minus)
                lines.append(jnp.where(first, gap, -gap))
        for m, line in enumerate(lines):
            at = start + 2 * half * m
            send_a[:, at:at + 2 * half] = line.astype(jnp.bfloat16)
        for to in others_g:
            sums_copy(k, to).start()
        own = pl.ds(pl.multiple_of(own_g * share, share), share)
        recv_a[own, start:start + width] = send_a[own, start:start + width]

    def cells_copy(k, to):
        start, width = spans[k]
        return pltpu.make_async_remote_copy(
            src_ref=send_b.at[to, :, pl.ds(start, width)],
            dst_ref=recv_b.at[own_b, :, pl.ds(start, width)],
            send_sem=b_send.at[k], recv_sem=b_recv.at[k],
            device_id=(own_g, to), device_id_type=MESH)

    def start_cells(k):
        start, width = spans[k]
        wait_for(recv_a.at[pl.ds(0, (groups - 1) * share), pl.ds(start, width)], a_recv.at[k])
        stacked = jnp.dot(matches[...], recv_a[:, start:start + width], preferred_element_type=jnp.float32)
        send_b[:, :, start:start + width] = stacked.astype(jnp.bfloat16).reshape(blocks, cells, width)
        for to in partners:
            cells_copy(k, to).start()
        recv_b[own_b, :, start:start + width] = send_b[own_b, :, start:start + width]

    def transform(k):
        start, width = spans[k]
        wait_for(recv_b.at[pl.ds(0, blocks - 1), :, pl.ds(start, width)], b_recv.at[k])
        lines = []
        for m in range(len(made[k])):
            at = start + 2 * half * m
            lines.append(jnp.concatenate([recv_b[b, :, at:at + 2 * half] for b in range(blocks)], axis=1))
        spectrum = jnp.concatenate(lines, axis=0) if len(lines) > 1 else lines[0]
        lag = jnp.dot(spectrum, table[...], preferred_element_type=jnp.float32).astype(jnp.bfloat16)
        for m, c in enumerate(made[k]):
            out_ref[c] = lag[m * cells:(m + 1) * cells]

    count = len(CHUNKS)
    for k in range(count):
        slot_sums(k)
        start_sums(k)
    table_copy.wait()
    wait_for(others, x_send)
    for k in range(count):
        start_cells(k)
    for k in range(count - 1):
        transform(k)
    for k in range(count):
        start, width = spans[k]
        wait_for(send_a.at[pl.ds(0, (groups - 1) * share), pl.ds(start, width)], a_send.at[k])
        if k < count - 1:
            wait_for(send_b.at[pl.ds(0, blocks - 1), :, pl.ds(start, width)], b_send.at[k])
    transform(count - 1)
    start, width = spans[count - 1]
    wait_for(send_b.at[pl.ds(0, blocks - 1), :, pl.ds(start, width)], b_send.at[count - 1])


def on_device(spectra, pair_slot, slot_cell, cell_rank):
    rows, _, _, freqs = spectra.shape
    groups, slot_count = slot_cell.shape
    blocks = lax.axis_size("partner")
    sensors = rows * blocks
    cells = cell_rank.shape[0] // (groups * blocks)
    own_bins = 2 * freqs // blocks
    width = 9 * own_bins
    share = slot_count // groups

    table = jnp.asarray(lag_table(freqs, blocks))
    count = len(CHUNKS)
    widest = max(len(chunk) for chunk in CHUNKS) * own_bins
    vmem = pl.BlockSpec(memory_space=pltpu.VMEM)
    out = pl.pallas_call(
        functools.partial(kernel, (groups, blocks, rows, cells)),
        out_shape=pltpu.VMEM((9, cells, 2 * freqs), jnp.bfloat16),
        in_specs=[pl.BlockSpec(memory_space=pl.ANY)] * 5,
        out_specs=vmem,
        scratch_shapes=[
            pltpu.VMEM(spectra.shape, spectra.dtype),
            pltpu.VMEM(pair_slot.shape, pair_slot.dtype),
            pltpu.VMEM(slot_cell.shape, slot_cell.dtype),
            pltpu.VMEM((cell_rank.shape[0] // 128, 128), cell_rank.dtype),
            pltpu.SemaphoreType.DMA((4,)),
            pltpu.VMEM((blocks, 4, rows, own_bins), jnp.bfloat16),
            pltpu.VMEM((blocks, 4, rows, own_bins), jnp.bfloat16),
            pltpu.VMEM((12, sensors, own_bins), jnp.float32),
            pltpu.VMEM((8, sensors + sensors // 2, own_bins), jnp.bfloat16),
            pltpu.VMEM((2, sensors // 2, sensors), jnp.float32),
            pltpu.VMEM((2, rows * rows // sensors, blocks, sensors), jnp.float32),
            pltpu.VMEM((2, slot_count, widest), jnp.float32),
            pltpu.VMEM((blocks * cells, groups * share), jnp.bfloat16),
            pltpu.VMEM((2 * freqs, 2 * freqs), jnp.bfloat16),
            pltpu.VMEM((slot_count, width), jnp.bfloat16),
            pltpu.VMEM((groups * share, width), jnp.bfloat16),
            pltpu.VMEM((blocks, cells, width), jnp.bfloat16),
            pltpu.VMEM((blocks, cells, width), jnp.bfloat16),
            pltpu.SemaphoreType.DMA,
            pltpu.SemaphoreType.DMA,
            pltpu.SemaphoreType.DMA,
            pltpu.SemaphoreType.DMA((count,)),
            pltpu.SemaphoreType.DMA((count,)),
            pltpu.SemaphoreType.DMA((count,)),
            pltpu.SemaphoreType.DMA((count,)),
        ],
        compiler_params=pltpu.CompilerParams(
            collective_id=0, has_side_effects=True, vmem_limit_bytes=56 * 2**20),
        name="stack_pairs",
    )(spectra, pair_slot, slot_cell, cell_rank.reshape(-1, 128), table)
    return out.transpose(1, 0, 2)


def solution(mesh):
    in_specs = (
        P(("sensor", "partner"), None, None, None),
        P(("sensor", "partner"), None),
        P(),
        P(),
    )
    out_specs = P(("sensor", "partner"), None, None)
    return jax.shard_map(
        on_device, mesh=mesh, in_specs=in_specs, out_specs=out_specs, check_vma=False
    )
```

```python
import functools
import math

import jax
import jax.numpy as jnp
import numpy as np
from jax import lax
from jax.experimental import pallas as pl
from jax.experimental.pallas import tpu as pltpu
from jax.sharding import PartitionSpec as P

MESH = pl.DeviceIdType.MESH
CHUNKS = (((0, 1), (0, 2)), ((1, 2), "01"), ("2",))
MADE = {(0, 1): (1, 3), (0, 2): (2, 6), (1, 2): (5, 7), "01": (0, 4), "2": (8,)}


def lag_table(freqs, blocks):
    lags = 2 * freqs
    bins = np.arange(freqs)[:, None]
    shifts = np.arange(lags)[None, :] - lags // 2
    angle = np.mod(bins * shifts, lags) * (2.0 * math.pi / lags)
    both = np.stack([np.cos(angle), -np.sin(angle)]) / freqs
    both = both.reshape(2, blocks, freqs // blocks, lags).transpose(1, 0, 2, 3)
    return both.reshape(2 * freqs, lags).astype(jnp.bfloat16)


def one_hot(condition):
    return jnp.where(condition, 1.0, 0.0).astype(jnp.bfloat16)


def cell_rows(slot_cell, rank_table, own_g, share, blocks, cells):
    groups, slot_count = slot_cell.shape
    span = rank_table.shape[1]
    count = groups * share
    of_slot = lax.broadcasted_iota(jnp.int32, (slot_count, count), 0)
    incoming = lax.broadcasted_iota(jnp.int32, (slot_count, count), 1)
    pick = one_hot(of_slot == own_g * share + incoming % share)
    used = slot_cell >= 0
    high = jnp.where(used, slot_cell // span, -1).astype(jnp.float32).astype(jnp.bfloat16)
    low = jnp.where(used, slot_cell % span, 0).astype(jnp.float32).astype(jnp.bfloat16)
    group = lax.broadcasted_iota(jnp.int32, (groups, count), 0)
    mine = group == lax.broadcasted_iota(jnp.int32, (groups, count), 1) // share

    def own(values):
        spread = jnp.dot(values, pick, preferred_element_type=jnp.float32)
        return jnp.sum(jnp.where(mine, spread, 0.0), axis=0, keepdims=True)

    high, low = own(high), own(low)
    place = (rank_table % cells).astype(jnp.float32).astype(jnp.bfloat16)
    low_ids = lax.broadcasted_iota(jnp.int32, (span, count), 0).astype(jnp.float32)
    spread = jnp.dot(place, one_hot(low_ids == low), preferred_element_type=jnp.float32)
    high_ids = lax.broadcasted_iota(jnp.int32, (rank_table.shape[0], count), 0).astype(jnp.float32)
    place = jnp.sum(jnp.where(high_ids == high, spread, 0.0), axis=0, keepdims=True)
    owner = lax.broadcasted_iota(jnp.int32, (1, count), 1) % share // (share // blocks)
    return jnp.where(high >= 0, place + (owner * cells).astype(jnp.float32), -1.0)


def wait_for(ref, semaphore):
    pltpu.make_async_copy(ref, ref, semaphore).wait()


def kernel(sizes, spectra_hbm, pair_slot_hbm, slot_cell_hbm, rank_hbm, table_hbm, out_ref, spectra_ref, pair_slot_ref,
           slot_cell_ref, rank_ref, in_sems, mine, got, left, right, slots,
           opposite, total, matches, table, send_a, recv_a, send_b, recv_b, table_sem,
           x_send, x_recv, a_send, a_recv, b_send, b_recv):
    groups, blocks, rows, cells = sizes
    sensors = blocks * rows
    own_g, own_b = lax.axis_index("sensor"), lax.axis_index("partner")
    inputs = [
        pltpu.make_async_copy(source, to, in_sems.at[n])
        for n, (source, to) in enumerate((
            (spectra_hbm, spectra_ref), (pair_slot_hbm, pair_slot_ref), (slot_cell_hbm, slot_cell_ref), (rank_hbm, rank_ref)))
    ]
    for copy in inputs:
        copy.start()
    half = out_ref.shape[2] // blocks // 2

    partners = [lax.rem(own_b + step, blocks) for step in sorted(range(1, blocks), key=lambda n: abs(n - blocks // 2))]
    side = math.isqrt(groups)
    hops = sorted(range(1, groups), key=lambda n: abs(n // side - side // 2) + abs(n % side - side // 2))
    others_g = [
        lax.rem(own_g // side + n // side, side) * side + lax.rem(lax.rem(own_g, side) + n % side, side) for n in hops
    ]
    barrier = pltpu.get_barrier_semaphore()
    for to in partners:
        pl.semaphore_signal(barrier, inc=1, device_id=(own_g, to), device_id_type=MESH)
    for to in others_g:
        pl.semaphore_signal(barrier, inc=1, device_id=(to, own_b), device_id_type=MESH)
    table_copy = pltpu.make_async_copy(table_hbm, table, table_sem)
    table_copy.start()

    for copy in inputs:
        copy.wait()
    ids = pair_slot_ref[...].astype(jnp.float32).astype(jnp.bfloat16)
    first = lax.broadcasted_iota(jnp.int32, (rows, 2 * half), 1) < half
    for a in range(3):
        for pair in range(blocks // 2):
            lanes = slice(pair * 2 * half, (pair + 1) * 2 * half)
            real = spectra_ref[:, a, 0, lanes].astype(jnp.float32)
            imag = spectra_ref[:, a, 1, lanes].astype(jnp.float32)
            mine[2 * pair, a] = jnp.where(first, real, pltpu.roll(imag, half, 1)).astype(jnp.bfloat16)
            mine[2 * pair + 1, a] = jnp.where(first, pltpu.roll(real, half, 1), imag).astype(jnp.bfloat16)
    for b in range(blocks):
        mine[b, 3] = ids
    share = slot_cell_ref.shape[1] // groups
    at = cell_rows(slot_cell_ref[...], rank_ref[...], own_g, share, blocks, cells)
    row_ids = lax.broadcasted_iota(jnp.int32, (blocks * cells, groups * share), 0).astype(jnp.float32)
    matches[...] = one_hot(row_ids == at)
    pl.semaphore_wait(barrier, blocks + groups - 2)

    def bins_copy(to):
        return pltpu.make_async_remote_copy(
            src_ref=mine.at[to], dst_ref=got.at[own_b], send_sem=x_send, recv_sem=x_recv,
            device_id=(own_g, to), device_id_type=MESH)

    for to in partners:
        bins_copy(to).start()
    got[own_b] = mine[own_b]
    others = got.at[pl.ds(0, blocks - 1)]
    wait_for(others, x_recv)

    low = lax.broadcasted_iota(jnp.int32, (sensors, 2 * half), 1) < half
    wrap = right.shape[1] - sensors
    plain, swapped = [], []
    for a in range(3):
        x = got[:, a].reshape(sensors, 2 * half).astype(jnp.float32)
        plain.append(x)
        swapped.append(pltpu.roll(x, half, 1))

    def keep_right(n, x):
        x = x.astype(jnp.bfloat16)
        right[n, :sensors] = x
        right[n, sensors:] = x[:wrap]

    for a in range(3):
        x, y = plain[a], swapped[a]
        left[a] = x
        left[3 + a] = jnp.where(low, y, -y)
        if a > 0:
            left[5 + a] = jnp.where(low, x, -x)
            left[7 + a] = y
        keep_right(a, jnp.where(low, x, y))
        keep_right(3 + a, jnp.where(low, y, x))
    real = jnp.where(low, plain[0], swapped[1])
    imag = jnp.where(low, swapped[0], plain[1])
    left[10] = real
    left[11] = imag
    keep_right(6, real)
    keep_right(7, imag)

    window = sensors // 2
    table_of_slots = got[:, 3].reshape(sensors, sensors).astype(jnp.float32)
    lane = lax.broadcasted_iota(jnp.int32, (window, sensors), 1)
    pick = one_hot(lax.broadcasted_iota(jnp.int32, (sensors, rows * rows), 0)
                   == window + lax.broadcasted_iota(jnp.int32, (sensors, rows * rows), 1) % rows)
    keep = (lax.broadcasted_iota(jnp.int32, (window, rows * rows), 0) % rows
            == lax.broadcasted_iota(jnp.int32, (window, rows * rows), 1) // rows)
    for n, ordered in enumerate((table_of_slots, table_of_slots.T)):
        turned = jnp.concatenate([
            ordered[b * rows:(b + 1) * rows] if b == 0
            else pltpu.roll(ordered[b * rows:(b + 1) * rows], sensors - b * rows, 1) for b in range(blocks)], axis=0)
        joined = jnp.where(lane < window, turned[:window], pltpu.roll(turned[window:], window, 1))
        if n == 1:
            joined = jnp.where(lane % window < rows, -1.0, joined)
        slots[n] = joined
        spread = jnp.dot(turned[:window].astype(jnp.bfloat16), pick, preferred_element_type=jnp.float32)
        spread = jnp.where(keep, spread, 0.0)
        for b in range(blocks // 2):
            line = jnp.sum(spread[b * rows:(b + 1) * rows], axis=0, keepdims=True)
            for m in range(rows * rows // sensors):
                opposite[n, m, b:b + 1] = line[:, m * sensors:(m + 1) * sensors]

    slot_count = total.shape[1]
    slot_ids = lax.broadcasted_iota(jnp.int32, (slot_count, sensors), 0).astype(jnp.float32).astype(jnp.bfloat16)

    def select(row):
        row = jnp.broadcast_to(row, (16, sensors)).astype(jnp.bfloat16)
        row = jnp.concatenate([row] * (slot_count // 16), axis=0)
        return jnp.where(row == slot_ids, jnp.bfloat16(1), jnp.bfloat16(0))

    def slot_sums(k):
        chunk = CHUNKS[k]
        width = 2 * half * len(chunk)

        def factors(i, term, count):
            def wide(n):
                one = jnp.broadcast_to(left[n, pl.ds(i, 1), :], (16, 2 * half)).astype(jnp.bfloat16)
                return jnp.concatenate([one] * (count // 16), axis=0) if count > 16 else one

            if term == "01":
                return wide(10), wide(11)
            if term == "2":
                return wide(2), wide(5)
            a, b = term
            return wide(a), wide(3 + a), wide(5 + b), wide(7 + b)

        def products(i, at, count, term):
            of = factors(i, term, count)
            there = pl.ds(at, count)
            if term == "01":
                real, imag = right[6, there, :], right[7, there, :]
                return of[0] * real + of[1] * imag, of[1] * real - of[0] * imag
            if term == "2":
                both = of[0] * right[2, there, :] + of[1] * right[5, there, :]
                return both, both
            a, b = term
            one = of[0] * right[b, there, :] + of[1] * right[3 + b, there, :]
            two = of[2] * right[a, there, :] + of[3] * right[3 + a, there, :]
            return one + two, one - two

        def add(step, carried):
            start = pl.multiple_of(step * rows, rows)
            half_on = pl.multiple_of(step * rows + window, rows)
            added, taken = [], []
            pieces = [(start + u, start, window) for u in range(rows)], [(half_on + u, half_on, window) for u in range(rows)]
            order = [piece for both in zip(*pieces) for piece in both]
            order += [(start + u, half_on, rows) for u in range(rows)]
            for i, at, count in order:
                terms = [products(i, at, count, term) for term in chunk]
                added.append(jnp.concatenate([t[0] for t in terms], axis=1))
                taken.append(jnp.concatenate([t[1] for t in terms], axis=1))
            sums, differences = [], []
            for u in range(rows + rows * rows // sensors):
                if u < rows:
                    a, b = (select(slots[n, pl.ds(start + u, 1), :]) for n in range(2))
                else:
                    a, b = (select(opposite[n, u - rows, pl.ds(step, 1), :]) for n in range(2))
                sums.append(a + b)
                differences.append(a - b)
            for n, (chosen, values) in enumerate(((sums, added), (differences, taken))):
                total[n, :, :width] += jnp.dot(
                    jnp.concatenate(chosen, axis=1), jnp.concatenate(values, axis=0), preferred_element_type=jnp.float32)
            return carried

        total[:, :, :width] = jnp.zeros((2, slot_count, width), jnp.float32)
        lax.fori_loop(0, blocks // 2, add, 0, unroll=4)

    made = [tuple(c for term in chunk for c in MADE[term]) for chunk in CHUNKS]
    spans = []
    begin = 0
    for pairs in made:
        spans.append((begin, 2 * half * len(pairs)))
        begin += 2 * half * len(pairs)

    def sums_copy(k, to):
        start, width = spans[k]
        return pltpu.make_async_remote_copy(
            src_ref=send_a.at[pl.ds(pl.multiple_of(to * share, share), share), pl.ds(start, width)],
            dst_ref=recv_a.at[pl.ds(pl.multiple_of(own_g * share, share), share), pl.ds(start, width)],
            send_sem=a_send.at[k], recv_sem=a_recv.at[k],
            device_id=(to, own_b), device_id_type=MESH)

    def start_sums(k):
        start, width = spans[k]
        first = lax.broadcasted_iota(jnp.int32, (slot_count, 2 * half), 1) < half
        lines = []
        for m, term in enumerate(CHUNKS[k]):
            plus, minus = (total[n, :, 2 * half * m:2 * half * (m + 1)] for n in range(2))
            if term == "2":
                lines.append(jnp.where(first, plus, minus))
            elif term == "01":
                lines.append(jnp.where(first, plus, pltpu.roll(minus, half, 1)))
                lines.append(jnp.where(first, pltpu.roll(plus, half, 1), minus))
            else:
                lines.append(0.5 * (plus + minus))
                gap = 0.5 * (plus - minus)
                lines.append(jnp.where(first, gap, -gap))
        for m, line in enumerate(lines):
            at = start + 2 * half * m
            send_a[:, at:at + 2 * half] = line.astype(jnp.bfloat16)
        for to in others_g:
            sums_copy(k, to).start()
        own = pl.ds(pl.multiple_of(own_g * share, share), share)
        recv_a[own, start:start + width] = send_a[own, start:start + width]

    def cells_copy(k, to):
        start, width = spans[k]
        return pltpu.make_async_remote_copy(
            src_ref=send_b.at[to, :, pl.ds(start, width)],
            dst_ref=recv_b.at[own_b, :, pl.ds(start, width)],
            send_sem=b_send.at[k], recv_sem=b_recv.at[k],
            device_id=(own_g, to), device_id_type=MESH)

    def start_cells(k):
        start, width = spans[k]
        wait_for(recv_a.at[pl.ds(0, (groups - 1) * share), pl.ds(start, width)], a_recv.at[k])
        stacked = jnp.dot(matches[...], recv_a[:, start:start + width], preferred_element_type=jnp.float32)
        send_b[:, :, start:start + width] = stacked.astype(jnp.bfloat16).reshape(blocks, cells, width)
        for to in partners:
            cells_copy(k, to).start()
        recv_b[own_b, :, start:start + width] = send_b[own_b, :, start:start + width]

    def transform(k):
        start, width = spans[k]
        wait_for(recv_b.at[pl.ds(0, blocks - 1), :, pl.ds(start, width)], b_recv.at[k])
        lines = []
        for m in range(len(made[k])):
            at = start + 2 * half * m
            lines.append(jnp.concatenate([recv_b[b, :, at:at + 2 * half] for b in range(blocks)], axis=1))
        spectrum = jnp.concatenate(lines, axis=0) if len(lines) > 1 else lines[0]
        lag = jnp.dot(spectrum, table[...], preferred_element_type=jnp.float32).astype(jnp.bfloat16)
        for m, c in enumerate(made[k]):
            out_ref[c] = lag[m * cells:(m + 1) * cells]

    count = len(CHUNKS)
    for k in range(count):
        slot_sums(k)
        start_sums(k)
    table_copy.wait()
    wait_for(others, x_send)
    start_cells(0)
    start_cells(2)
    start_cells(1)
    transform(0)
    transform(2)
    for k in range(count):
        start, width = spans[k]
        wait_for(send_a.at[pl.ds(0, (groups - 1) * share), pl.ds(start, width)], a_send.at[k])
        if k != 1:
            wait_for(send_b.at[pl.ds(0, blocks - 1), :, pl.ds(start, width)], b_send.at[k])
    transform(1)
    start, width = spans[1]
    wait_for(send_b.at[pl.ds(0, blocks - 1), :, pl.ds(start, width)], b_send.at[1])


def on_device(spectra, pair_slot, slot_cell, cell_rank):
    rows, _, _, freqs = spectra.shape
    groups, slot_count = slot_cell.shape
    blocks = lax.axis_size("partner")
    sensors = rows * blocks
    cells = cell_rank.shape[0] // (groups * blocks)
    own_bins = 2 * freqs // blocks
    width = 9 * own_bins
    share = slot_count // groups

    table = jnp.asarray(lag_table(freqs, blocks))
    count = len(CHUNKS)
    widest = max(len(chunk) for chunk in CHUNKS) * own_bins
    vmem = pl.BlockSpec(memory_space=pltpu.VMEM)
    out = pl.pallas_call(
        functools.partial(kernel, (groups, blocks, rows, cells)),
        out_shape=pltpu.VMEM((9, cells, 2 * freqs), jnp.bfloat16),
        in_specs=[pl.BlockSpec(memory_space=pl.ANY)] * 5,
        out_specs=vmem,
        scratch_shapes=[
            pltpu.VMEM(spectra.shape, spectra.dtype),
            pltpu.VMEM(pair_slot.shape, pair_slot.dtype),
            pltpu.VMEM(slot_cell.shape, slot_cell.dtype),
            pltpu.VMEM((cell_rank.shape[0] // 128, 128), cell_rank.dtype),
            pltpu.SemaphoreType.DMA((4,)),
            pltpu.VMEM((blocks, 4, rows, own_bins), jnp.bfloat16),
            pltpu.VMEM((blocks, 4, rows, own_bins), jnp.bfloat16),
            pltpu.VMEM((12, sensors, own_bins), jnp.float32),
            pltpu.VMEM((8, sensors + sensors // 2, own_bins), jnp.bfloat16),
            pltpu.VMEM((2, sensors // 2, sensors), jnp.float32),
            pltpu.VMEM((2, rows * rows // sensors, blocks, sensors), jnp.float32),
            pltpu.VMEM((2, slot_count, widest), jnp.float32),
            pltpu.VMEM((blocks * cells, groups * share), jnp.bfloat16),
            pltpu.VMEM((2 * freqs, 2 * freqs), jnp.bfloat16),
            pltpu.VMEM((slot_count, width), jnp.bfloat16),
            pltpu.VMEM((groups * share, width), jnp.bfloat16),
            pltpu.VMEM((blocks, cells, width), jnp.bfloat16),
            pltpu.VMEM((blocks, cells, width), jnp.bfloat16),
            pltpu.SemaphoreType.DMA,
            pltpu.SemaphoreType.DMA,
            pltpu.SemaphoreType.DMA,
            pltpu.SemaphoreType.DMA((count,)),
            pltpu.SemaphoreType.DMA((count,)),
            pltpu.SemaphoreType.DMA((count,)),
            pltpu.SemaphoreType.DMA((count,)),
        ],
        compiler_params=pltpu.CompilerParams(
            collective_id=0, has_side_effects=True, vmem_limit_bytes=56 * 2**20),
        name="stack_pairs",
    )(spectra, pair_slot, slot_cell, cell_rank.reshape(-1, 128), table)
    return out.transpose(1, 0, 2)


def solution(mesh):
    in_specs = (
        P(("sensor", "partner"), None, None, None),
        P(("sensor", "partner"), None),
        P(),
        P(),
    )
    out_specs = P(("sensor", "partner"), None, None)
    return jax.shard_map(
        on_device, mesh=mesh, in_specs=in_specs, out_specs=out_specs, check_vma=False
    )
```
